512 devices in a mesh: dp: 8 (over y), ctx: 16 (over z_hi, x, core), head: 4 (over z_lo).
Axes of the slice: x: 4, y: 8, z: 8 (z_hi: 2, z_lo: 4; z = z_hi * 4 + z_lo), core: 2. Of those that a mesh axis runs over, the one named last changes fastest.
Arguments:
- queries: bfloat16 [65536, 3072], P(('dp', 'ctx'), 'head'), parts along dimension 0, may hold values from -6 to 6
- keys: bfloat16 [65536, 3072], P(('dp', 'ctx'), 'head'), parts along dimension 0, may hold values from -8 to 8
- values: bfloat16 [65536, 3072], P(('dp', 'ctx'), 'head'), parts along dimension 0, may hold values from -8 to 8
- pool_segments: int32 [128, 512], P(('dp', 'ctx')), parts along dimension 0, may hold values from 0 to 7, never falling along the last dimension, each value on 1 to 96 neighbouring positions
- window_map: int32 [128], P(('dp', 'ctx')), parts along dimension 0, may hold values from 0 to 15, each once
- ref_owner: int32 [8], P('dp'), parts along dimension 0, may hold values from 0 to 15
- ref_keys: bfloat16 [128, 512, 3072], P(('dp', 'ctx'), 'head'), parts along dimension 0, may hold values from -6 to 6
- ref_values: bfloat16 [128, 512, 3072], P(('dp', 'ctx'), 'head'), parts along dimension 0, may hold values from -6 to 6
- slopes: float32 [24], P('head'), may hold values from 0.02 to 2
Outputs:
- attended: bfloat16 [65536, 3072], P(('dp', 'ctx'), 'head'), parts along dimension 0
The draws below stay inside these ranges and needn't reach their ends.
There are 8 independent parts, one for each index of `dp`. The reference program is written for one: setup_inputs(seed, part) draws one part's arguments, and reference() takes and returns one part's arrays. A program takes and returns all parts, laid end to end along the dimension named above; an argument that names none is the same for every part. Nothing has to cross between parts.
All inputs are finite; a program needn't handle non-finite values.
Results may differ from the reference program's by a relative error of at most 0.0021.
Values may be sent and summed in bfloat16 or wider, within the bound.
No kernel may reach another device: no remote copies, remote signals or barrier semaphores. Data moves between devices by JAX's collectives and lax.ppermute only.
A program may use at most 64 MiB of HBM per device.

```python
import math
from functools import reduce
import jax
import jax.numpy as jnp
import numpy as np
from jax import lax

HEADS = 24
HD = 128
D = 3072
TOK_DEV = 512
RATIO = 64
POOLS = 8
POOL_MOST = 96
REF = 512
TOKENS = 8192
N_CTX = 16


def draw_queries(key, part):
    key = jax.random.fold_in(key, 11)
    base_draw = jnp.clip(jax.random.normal(key, (TOKENS, D), jnp.float32), -6.0, 6.0)
    return base_draw.astype(jnp.bfloat16)


def draw_keys(key, part):
    key = jax.random.fold_in(key, 23)
    slow_key, fast_key = jax.random.split(key)
    slow_part = jax.random.normal(slow_key, (TOKENS // RATIO, D), jnp.float32)
    fast_part = jax.random.normal(fast_key, (TOKENS, D), jnp.float32)
    base_draw = 1.5 * jnp.repeat(slow_part, RATIO, axis=0) + fast_part
    return jnp.clip(base_draw, -8.0, 8.0).astype(jnp.bfloat16)


def draw_values(key, part):
    key = jax.random.fold_in(key, 37)
    slow_key, fast_key = jax.random.split(key)
    slow_part = jax.random.normal(slow_key, (TOKENS // RATIO, D), jnp.float32)
    fast_part = jax.random.normal(fast_key, (TOKENS, D), jnp.float32)
    base_draw = 1.5 * jnp.repeat(slow_part, RATIO, axis=0) + fast_part
    return jnp.clip(base_draw, -8.0, 8.0).astype(jnp.bfloat16)


def level_of(rng, shape, pieces, smallest, largest):
    factor_of = 1.0
    for dim, shards_of in pieces:
        heights = jax.random.uniform(jax.random.fold_in(jax.random.fold_in(rng, 6), dim), (shards_of,), jnp.float32, smallest / len(pieces), largest / len(pieces))
        factor_of = factor_of * jnp.repeat(jnp.exp(heights), shape[dim] // shards_of).reshape((-1,) + (1,) * (len(shape) - 1 - dim))
    return factor_of


def profile(number_of, total, bound, lean):
    portions = [(1 << 20) // math.isqrt(standing ** lean) + 1 for standing in range(2, number_of + 1)]
    spare, holding = total - bound - (number_of - 1), [1] * (number_of - 1)
    while spare > 0:
        candidates = [i for i in range(number_of - 1) if holding[i] < bound]
        mass, left = sum([portions[i] for i in candidates]), spare
        for i in candidates:
            addition = min(bound - holding[i], max(1, left * portions[i] // mass), spare)
            holding[i] = holding[i] + addition
            spare = spare - addition
    return np.array([bound] + holding)


def ragged_sizes(own_key, number_of, total, reach, lean):
    if number_of == 2:
        one = jax.random.randint(own_key, (), max(1, total - reach), min(reach, total - 1) + 1)
        return jnp.stack([one, total - one])
    sizes = jnp.asarray(profile(number_of, total, reach, lean), jnp.int32)
    twos = (number_of - 1) // 2
    giver, receiver = sizes[1:1 + 2 * twos:2], sizes[2:2 + 2 * twos:2]
    room = jnp.minimum(giver - 1, reach - receiver)
    passed = jax.random.randint(jax.random.fold_in(own_key, 1), (twos,), 0, 1 << 20) % (room + 1)
    sizes = sizes.at[1:1 + 2 * twos:2].set(giver - passed).at[2:2 + 2 * twos:2].set(receiver + passed)
    return sizes[jax.random.permutation(jax.random.fold_in(own_key, 2), number_of)]


def centred(key, extent, scale, bound, cuts=(), kind=jnp.bfloat16):
    gain = level_of(key, extent, cuts, -0.22, 0.18) if cuts else 1.0
    result = jax.random.normal(key, extent, jnp.float32) * scale * gain
    return jnp.minimum(jnp.maximum(result, -bound), bound).astype(kind)


def setup_inputs(seed: int = 0, part: int = 0) -> dict:
    arg_keys = jax.random.split(jax.random.key(seed), 10)
    part_keys = jax.random.split(jax.random.fold_in(arg_keys[9], part), 10)
    return {
        "queries": draw_queries(jax.random.fold_in(jax.random.fold_in(arg_keys[9], part), 71), part),
        "keys": draw_keys(jax.random.fold_in(jax.random.fold_in(arg_keys[9], part), 71), part),
        "values": draw_values(jax.random.fold_in(jax.random.fold_in(arg_keys[9], part), 71), part),
        "pool_segments": jax.vmap(lambda own: jnp.searchsorted(jnp.cumsum(ragged_sizes(own, POOLS, TOK_DEV, POOL_MOST, 0)), jnp.arange(TOK_DEV), side="right"))(jax.random.split(part_keys[3], N_CTX)).reshape((N_CTX, TOK_DEV)).astype(jnp.int32),
        "window_map": jax.random.permutation(part_keys[4], N_CTX).astype(jnp.int32),
        "ref_owner": jax.random.randint(part_keys[5], (1,), 0, N_CTX).astype(jnp.int32),
        "ref_keys": centred(part_keys[6], (N_CTX, REF, D), 1.0, 6.0, ((0, 16), (1, 4))),
        "ref_values": centred(part_keys[7], (N_CTX, REF, D), 1.0, 6.0, ((0, 16), (1, 4))),
        "slopes": jnp.clip(jnp.exp(math.log(2.0) - 4.6051702 * jax.random.uniform(arg_keys[8], (HEADS,), jnp.float32) ** level_of(arg_keys[8], (HEADS,), ((0, 4),), -0.2, 0.2)), 0.02, 2.0),
    }


def group_terms(query_block, key_block, value_block, bias_term):
    score_scale = 1.0 / math.sqrt(HD)
    scores = jnp.einsum('qhd,khd->hqk', query_block.astype(jnp.float32), key_block.astype(jnp.float32)) * score_scale
    if bias_term is not None:
        scores = scores + bias_term[:, None, :]
    row_max = lax.optimization_barrier(jnp.max(scores, axis=2))
    exp_terms = jnp.exp(scores - row_max[:, :, None])
    row_total = lax.optimization_barrier(jnp.sum(exp_terms, axis=2))
    weights = exp_terms.astype(jnp.bfloat16)
    numerator = jnp.einsum('hqk,khd->qhd', weights.astype(jnp.float32), value_block.astype(jnp.float32))
    return (row_max.T, row_total.T, numerator)

def combine_groups(group_list):
    ceiling = reduce(jnp.maximum, [triple[0] for triple in group_list])
    numerator = reduce(jnp.add, [jnp.exp(triple[0] - ceiling)[:, :, None] * triple[2] for triple in group_list])
    denominator = reduce(jnp.add, [jnp.exp(triple[0] - ceiling) * triple[1] for triple in group_list])
    return numerator / denominator[:, :, None]

def reference(queries, keys, values, pool_segments, window_map, ref_owner, ref_keys, ref_values, slopes):
    member = (pool_segments[:, None, :] == jnp.arange(POOLS, dtype=jnp.int32)[None, :, None]).astype(jnp.float32)
    counts = lax.optimization_barrier(jnp.sum(member, axis=2))
    key_blocks = keys.reshape(N_CTX, TOK_DEV, D).astype(jnp.float32)
    value_blocks = values.reshape(N_CTX, TOK_DEV, D).astype(jnp.float32)
    pooled_keys = (jnp.einsum('bpt,btf->bpf', member, key_blocks) / counts[:, :, None]).astype(jnp.bfloat16)
    pooled_values = (jnp.einsum('bpt,btf->bpf', member, value_blocks) / counts[:, :, None]).astype(jnp.bfloat16)
    pooled_keys = pooled_keys.reshape(N_CTX * POOLS, HEADS, HD)
    pooled_values = pooled_values.reshape(N_CTX * POOLS, HEADS, HD)
    window_float = window_map.astype(jnp.float32)
    key_window = jnp.repeat(window_float, POOLS)
    ref_index = ref_owner[0].astype(jnp.int32)
    ref_k = lax.dynamic_index_in_dim(ref_keys, ref_index, 0, keepdims=False).reshape(REF, HEADS, HD)
    ref_v = lax.dynamic_index_in_dim(ref_values, ref_index, 0, keepdims=False).reshape(REF, HEADS, HD)

    def one_block(block_idx):
        start = (block_idx * TOK_DEV).astype(jnp.int32)
        query_block = lax.dynamic_slice_in_dim(queries, start, TOK_DEV, 0).reshape(TOK_DEV, HEADS, HD)
        key_block = lax.dynamic_slice_in_dim(keys, start, TOK_DEV, 0).reshape(TOK_DEV, HEADS, HD)
        value_block = lax.dynamic_slice_in_dim(values, start, TOK_DEV, 0).reshape(TOK_DEV, HEADS, HD)
        distance = jnp.abs(window_float[block_idx] - key_window)
        bias_term = -slopes[:, None] * distance[None, :]
        group_list = [group_terms(query_block, key_block, value_block, None), group_terms(query_block, pooled_keys, pooled_values, bias_term), group_terms(query_block, ref_k, ref_v, None)]
        return combine_groups(group_list).reshape(TOK_DEV, D).astype(jnp.bfloat16)
    all_blocks = lax.map(one_block, jnp.arange(N_CTX, dtype=jnp.int32))
    return all_blocks.reshape(TOKENS, D)
```

```python
import math

import jax
import jax.numpy as jnp
from jax import lax
from jax.experimental import pallas as pl
from jax.experimental.pallas import tpu as pltpu
from jax.sharding import Mesh, PartitionSpec as P

HD = 128
POOLS = 8
LOG2E = math.log2(math.e)
UNIT = LOG2E / math.sqrt(HD)
ROWS = 128
SWAP = [(0, 1), (1, 0)]


def dot_nt(a, b):
    return lax.dot_general(a, b, (((1,), (1,)), ((), ())), preferred_element_type=jnp.float32)


def dot_nn(a, b):
    return jnp.dot(a, b, preferred_element_type=jnp.float32)


def pool_kernel(tag_ref, seg_ref, key_ref, value_ref, out_ref):
    seg = seg_ref[...]
    member = seg == lax.broadcasted_iota(jnp.int32, (POOLS, seg.shape[1]), 0)
    count = jnp.sum(member.astype(jnp.float32), axis=1, keepdims=True)
    member = member.astype(jnp.float32).astype(jnp.bfloat16)
    width = key_ref.shape[1]
    out_ref[:, :width] = (dot_nn(member, key_ref[...]) / count).astype(jnp.bfloat16)
    out_ref[:, width : 2 * width] = (dot_nn(member, value_ref[...]) / count).astype(jnp.bfloat16)
    tag = jnp.full((POOLS, HD), tag_ref[0], jnp.int32)
    out_ref[:, 2 * width :] = tag.astype(jnp.float32).astype(jnp.bfloat16)


def soft(scores):
    row_max = jnp.max(scores, axis=1, keepdims=True)
    exp_terms = jnp.exp2(scores - row_max)
    return row_max, jnp.sum(exp_terms, axis=1, keepdims=True), exp_terms.astype(jnp.bfloat16)


def near_kernel(tag_ref, slope_ref, q_ref, k_ref, v_ref, pk_ref, pv_ref, pt_ref, acc_ref, stat_ref):
    head = pl.program_id(0)
    tags = pt_ref[...].astype(jnp.float32).T[0:1, :]
    bias = jnp.abs(tags - tag_ref[0].astype(jnp.float32)) * (slope_ref[head] * LOG2E)
    lane = lax.broadcasted_iota(jnp.int32, (ROWS, HD), 1)

    @pl.when(head == 0)
    def _():
        stat_ref[...] = jnp.zeros_like(stat_ref)

    for start in range(0, q_ref.shape[0], ROWS):
        rows = pl.ds(start, ROWS)
        q = q_ref[rows, :]
        max_w, total_w, weight_w = soft(dot_nt(q, k_ref[...]) * UNIT)
        num_w = dot_nn(weight_w, v_ref[...])
        max_p, total_p, weight_p = soft(dot_nt(q, pk_ref[...]) * UNIT - bias)
        num_p = dot_nn(weight_p, pv_ref[...])
        top = jnp.maximum(max_w, max_p)
        share_w, share_p = jnp.exp2(max_w - top), jnp.exp2(max_p - top)
        acc_ref[rows, :] = share_w * num_w + share_p * num_p
        total = share_w * total_w + share_p * total_p
        stat = jnp.where(lane == 2 * head, top, stat_ref[rows, :])
        stat_ref[rows, :] = jnp.where(lane == 2 * head + 1, total, stat)


def ref_kernel(core_ref, q_ref, own_ref, got_ref, acc_ref, stat_ref, out_ref):
    head = pl.program_id(0)
    first = core_ref[0] == 0
    keys = jnp.where(first, own_ref[...], got_ref[...])
    values = jnp.where(first, got_ref[...], own_ref[...])
    lane = lax.broadcasted_iota(jnp.int32, (ROWS, HD), 1)
    for start in range(0, q_ref.shape[0], ROWS):
        rows = pl.ds(start, ROWS)
        max_r, total_r, weight_r = soft(dot_nt(q_ref[rows, :], keys) * UNIT)
        num_r = dot_nn(weight_r, values)
        stat = stat_ref[rows, :]
        max_n = jnp.sum(jnp.where(lane == 2 * head, stat, 0.0), axis=1, keepdims=True)
        total_n = jnp.sum(jnp.where(lane == 2 * head + 1, stat, 0.0), axis=1, keepdims=True)
        top = jnp.maximum(max_n, max_r)
        share_n, share_r = jnp.exp2(max_n - top), jnp.exp2(max_r - top)
        total = share_n * total_n + share_r * total_r
        num = share_n * acc_ref[rows, :] + share_r * num_r
        out_ref[rows, :] = (num / total).astype(jnp.bfloat16)


SMEM = pl.BlockSpec(memory_space=pltpu.SMEM)
VMEM = pl.BlockSpec(memory_space=pltpu.VMEM)


def on_device(
    queries, keys, values, pool_segments, window_map, ref_owner, ref_keys, ref_values, slopes
):
    rows, width = queries.shape
    heads = width // HD
    n_zh, n_x, n_head = lax.axis_size("zh"), lax.axis_size("x"), lax.axis_size("head")
    ref_rows = ref_keys.shape[1]
    part = ref_rows // n_x
    core = lax.axis_index("c")
    owner = ref_owner[0]
    owner_c = owner % 2
    owner_x = (owner // 2) % n_x
    owner_z = owner // (2 * n_x)

    slot_k, slot_v = ref_keys[0], ref_values[0]
    got_k = lax.ppermute(slot_k, "c", [(1, 0)])
    got_v = lax.ppermute(slot_v, "c", [(0, 1)])
    mine = jnp.where(
        core == 0,
        jnp.where(owner_c == 0, slot_k, got_k),
        jnp.where(owner_c == 1, slot_v, got_v),
    )
    spread = lax.all_to_all(mine.reshape(n_x, part, -1), "x", 0, 0, tiled=True)
    piece = lax.dynamic_index_in_dim(spread, owner_x, 0, keepdims=False)
    piece = piece.reshape(part, n_head, width).transpose(1, 0, 2)
    piece = jnp.broadcast_to(piece[None], (n_zh, n_head, part, width))
    turned = lax.all_to_all(
        piece.reshape(n_zh * n_head, part, width), ("zh", "head"), 0, 0, tiled=True
    )
    turned = turned.reshape(n_zh, n_head * part, width)
    block = lax.dynamic_index_in_dim(turned, owner_z, 0, keepdims=False)
    block = jnp.broadcast_to(block[None], (n_x, n_head * part, width))
    own = lax.all_to_all(block, "x", 0, 0, tiled=True).reshape(-1, width)
    got = lax.ppermute(own, "c", SWAP)

    pooled = pl.pallas_call(
        pool_kernel,
        out_shape=jax.ShapeDtypeStruct((POOLS, 2 * width + HD), jnp.bfloat16),
        in_specs=[SMEM, VMEM, VMEM, VMEM],
        out_specs=VMEM,
        name="pool",
    )(window_map, pool_segments, keys, values)

    def double(block, axis, pairs):
        return jnp.concatenate([block, lax.ppermute(block, axis, pairs)], axis=0)

    pooled = double(pooled, "zh", SWAP)
    pooled = double(pooled, "x", [(i, i ^ 1) for i in range(n_x)])
    pooled = double(pooled, "x", [(i, i ^ 2) for i in range(n_x)])
    pooled = double(pooled, "c", SWAP)
    count = pooled.shape[0]

    by_head = pl.BlockSpec((rows, HD), lambda h: (0, h))
    acc, stat = pl.pallas_call(
        near_kernel,
        grid=(heads,),
        out_shape=(
            jax.ShapeDtypeStruct((rows, width), jnp.float32),
            jax.ShapeDtypeStruct((rows, HD), jnp.float32),
        ),
        in_specs=[
            SMEM,
            SMEM,
            by_head,
            by_head,
            by_head,
            pl.BlockSpec((count, HD), lambda h: (0, h)),
            pl.BlockSpec((count, HD), lambda h: (0, heads + h)),
            pl.BlockSpec((count, HD), lambda h: (0, 2 * heads)),
        ],
        out_specs=(by_head, pl.BlockSpec((rows, HD), lambda h: (0, 0))),
        compiler_params=pltpu.CompilerParams(vmem_limit_bytes=32 * 1024 * 1024),
        name="near",
    )(window_map, slopes, queries, keys, values, pooled, pooled, pooled)

    ref_block = pl.BlockSpec((own.shape[0], HD), lambda h: (0, h))
    return pl.pallas_call(
        ref_kernel,
        grid=(heads,),
        out_shape=jax.ShapeDtypeStruct((rows, width), jnp.bfloat16),
        in_specs=[
            SMEM,
            by_head,
            ref_block,
            ref_block,
            by_head,
            pl.BlockSpec((rows, HD), lambda h: (0, 0)),
        ],
        out_specs=by_head,
        compiler_params=pltpu.CompilerParams(vmem_limit_bytes=32 * 1024 * 1024),
        name="far",
    )(core.astype(jnp.int32)[None], queries, own, got, acc, stat)


def solution(mesh):
    shape = mesh.shape
    ctx = shape["ctx"]
    fine = Mesh(
        mesh.devices.reshape(shape["dp"], 2, ctx // 4, 2, shape["head"]),
        ("dp", "zh", "x", "c", "head"),
    )
    token = ("dp", "zh", "x", "c")
    return jax.shard_map(
        on_device,
        mesh=fine,
        in_specs=(
            P(token, "head"),
            P(token, "head"),
            P(token, "head"),
            P(token, None),
            P(token),
            P("dp"),
            P(token, "head", None),
            P(token, "head", None),
            P("head"),
        ),
        out_specs=P(token, "head"),
        check_vma=False,
    )
```

```python
import math

import jax
import jax.numpy as jnp
from jax import lax
from jax.experimental import pallas as pl
from jax.experimental.pallas import tpu as pltpu
from jax.sharding import Mesh, PartitionSpec as P

HD = 128
POOLS = 8
LOG2E = math.log2(math.e)
UNIT = LOG2E / math.sqrt(HD)
STRIP = 128
SWAP = [(0, 1), (1, 0)]


def dot_nt(a, b):
    return lax.dot_general(a, b, (((1,), (1,)), ((), ())), preferred_element_type=jnp.float32)


def dot_nn(a, b):
    return jnp.dot(a, b, preferred_element_type=jnp.float32)


def pool_kernel(tag_ref, seg_ref, key_ref, value_ref, out_ref):
    seg = seg_ref[...]
    member = seg == lax.broadcasted_iota(jnp.int32, (POOLS, seg.shape[1]), 0)
    count = jnp.sum(member.astype(jnp.float32), axis=1, keepdims=True)
    member = member.astype(jnp.float32).astype(jnp.bfloat16)
    width = key_ref.shape[1]
    out_ref[:, :width] = (dot_nn(member, key_ref[...]) / count).astype(jnp.bfloat16)
    out_ref[:, width : 2 * width] = (dot_nn(member, value_ref[...]) / count).astype(jnp.bfloat16)
    tag = jnp.full((POOLS, HD), tag_ref[0], jnp.int32)
    out_ref[:, 2 * width :] = tag.astype(jnp.float32).astype(jnp.bfloat16)


def soft(scores):
    top = jnp.max(scores, axis=0, keepdims=True)
    exp_terms = jnp.exp2(scores - top)
    return top, jnp.sum(exp_terms, axis=0, keepdims=True), exp_terms.astype(jnp.bfloat16)


def window_kernel(q_ref, k_ref, v_ref, acc_ref, stat_ref):
    for head in range(q_ref.shape[1] // HD):
        cols = pl.ds(head * HD, HD)
        values = v_ref[:, cols].T
        for start in range(0, q_ref.shape[0], STRIP):
            rows = pl.ds(start, STRIP)
            top, total, weights = soft(dot_nt(k_ref[:, cols], q_ref[rows, cols]) * UNIT)
            acc_ref[cols, rows] = dot_nn(values, weights)
            stat_ref[2 * head : 2 * head + 1, rows] = top
            stat_ref[2 * head + 1 : 2 * head + 2, rows] = total


def pooled_kernel(tag_ref, slope_ref, q_ref, p_ref, acc_ref, stat_ref):
    count, width = q_ref.shape
    tags = p_ref[:, 2 * width :].astype(jnp.float32)
    dist = jnp.abs(tags - tag_ref[0].astype(jnp.float32)) * LOG2E
    dist = jnp.concatenate([dist] * (count // HD), axis=1)
    for head in range(width // HD):
        cols = pl.ds(head * HD, HD)
        scores = dot_nt(p_ref[:, cols], q_ref[:, cols]) * UNIT - dist * slope_ref[head]
        top, total, weights = soft(scores)
        acc_ref[cols, :] = dot_nn(p_ref[:, pl.ds(width + head * HD, HD)].T, weights)
        stat_ref[2 * head : 2 * head + 1, :] = top
        stat_ref[2 * head + 1 : 2 * head + 2, :] = total


def ref_kernel(
    core_ref, q_ref, own_ref, got_ref, acc_w_ref, stat_w_ref, acc_p_ref, stat_p_ref, out_ref
):
    first = core_ref[0] == 0
    for head in range(q_ref.shape[1] // HD):
        cols = pl.ds(head * HD, HD)
        top_at, total_at = slice(2 * head, 2 * head + 1), slice(2 * head + 1, 2 * head + 2)
        keys = jnp.where(first, own_ref[:, cols], got_ref[:, cols])
        values = jnp.where(first, got_ref[:, cols], own_ref[:, cols]).T
        for start in range(0, q_ref.shape[0], STRIP):
            rows = pl.ds(start, STRIP)
            top, total, weights = soft(dot_nt(keys, q_ref[rows, cols]) * UNIT)
            num = dot_nn(values, weights)
            top_w, top_p = stat_w_ref[top_at, rows], stat_p_ref[top_at, rows]
            ceiling = jnp.maximum(jnp.maximum(top_w, top_p), top)
            share_w, share_p = jnp.exp2(top_w - ceiling), jnp.exp2(top_p - ceiling)
            share = jnp.exp2(top - ceiling)
            scale = 1.0 / (
                share_w * stat_w_ref[total_at, rows]
                + share_p * stat_p_ref[total_at, rows]
                + share * total
            )
            merged = (
                (share_w * scale) * acc_w_ref[cols, rows]
                + (share_p * scale) * acc_p_ref[cols, rows]
                + (share * scale) * num
            )
            out_ref[rows, cols] = merged.astype(jnp.bfloat16).T


SMEM = pl.BlockSpec(memory_space=pltpu.SMEM)
VMEM = pl.BlockSpec(memory_space=pltpu.VMEM)


def on_device(
    queries, keys, values, pool_segments, window_map, ref_owner, ref_keys, ref_values, slopes
):
    rows, width = queries.shape
    heads = width // HD
    n_zh, n_x, n_head = lax.axis_size("zh"), lax.axis_size("x"), lax.axis_size("head")
    ref_rows = ref_keys.shape[1]
    part = ref_rows // n_x
    core = lax.axis_index("c")
    owner = ref_owner[0]
    owner_c = owner % 2
    owner_x = (owner // 2) % n_x
    owner_z = owner // (2 * n_x)

    tie = lax.optimization_barrier
    near = pltpu.CompilerParams(vmem_limit_bytes=16 * 1024 * 1024)
    state = (
        jax.ShapeDtypeStruct((width, rows), jnp.float32),
        jax.ShapeDtypeStruct((16, rows), jnp.float32),
    )

    slot_k, slot_v = ref_keys[0], ref_values[0]
    got_k = lax.ppermute(slot_k, "c", [(1, 0)])
    got_v = lax.ppermute(slot_v, "c", [(0, 1)])
    kept = tie(jnp.where(core == 0, slot_k, slot_v))
    pooled = pl.pallas_call(
        pool_kernel,
        out_shape=jax.ShapeDtypeStruct((POOLS, 2 * width + HD), jnp.bfloat16),
        in_specs=[SMEM, VMEM, VMEM, VMEM],
        out_specs=VMEM,
        name="pool",
    )(window_map, pool_segments, keys, values)
    mine = jnp.where(owner_c == core, kept, jnp.where(core == 0, got_k, got_v))
    mine, pooled = tie((mine, pooled))

    spread = lax.all_to_all(mine.reshape(n_x, part, -1), "x", 0, 0, tiled=True)
    other = lax.ppermute(pooled, "zh", SWAP)
    piece = lax.dynamic_index_in_dim(spread, owner_x, 0, keepdims=False)
    piece = piece.reshape(part, n_head, width).transpose(1, 0, 2)
    piece = jnp.broadcast_to(piece[None], (n_zh, n_head, part, width))
    piece, pooled, other = tie((piece, pooled, other))

    turned = lax.all_to_all(
        piece.reshape(n_zh * n_head, part, width), ("zh", "head"), 0, 0, tiled=True
    )
    pooled = jnp.concatenate([pooled, other], axis=0)
    other = lax.ppermute(pooled, "c", SWAP)
    pooled = jnp.concatenate([pooled, other], axis=0)
    other = lax.ppermute(pooled, "x", [(i, i ^ 1) for i in range(n_x)])
    pooled = jnp.concatenate([pooled, other], axis=0)
    turned = turned.reshape(n_zh, n_head * part, width)
    block = lax.dynamic_index_in_dim(turned, owner_z, 0, keepdims=False)
    block = jnp.broadcast_to(block[None], (n_x, n_head * part, width))
    block, pooled, queries_w = tie((block, pooled, queries))

    own = lax.all_to_all(block, "x", 0, 0, tiled=True).reshape(-1, width)
    other = lax.ppermute(pooled, "x", [(i, i ^ 2) for i in range(n_x)])
    acc_w, stat_w = pl.pallas_call(
        window_kernel,
        out_shape=state,
        in_specs=[VMEM] * 3,
        out_specs=(VMEM, VMEM),
        compiler_params=near,
        cost_estimate=pl.CostEstimate(
            flops=4 * rows * rows * width,
            bytes_accessed=10 * rows * width,
            transcendentals=rows * rows * heads,
        ),
        name="window",
    )(queries_w, keys, values)
    pooled = jnp.concatenate([pooled, other], axis=0)
    own, pooled, acc_w, stat_w = tie((own, pooled, acc_w, stat_w))

    got = lax.ppermute(own, "c", SWAP)
    acc_p, stat_p = pl.pallas_call(
        pooled_kernel,
        out_shape=state,
        in_specs=[SMEM, SMEM, VMEM, VMEM],
        out_specs=(VMEM, VMEM),
        compiler_params=near,
        cost_estimate=pl.CostEstimate(
            flops=4 * rows * pooled.shape[0] * width,
            bytes_accessed=6 * rows * width,
            transcendentals=rows * pooled.shape[0] * heads,
        ),
        name="pooled",
    )(window_map, slopes, queries, pooled)
    return pl.pallas_call(
        ref_kernel,
        out_shape=jax.ShapeDtypeStruct((rows, width), jnp.bfloat16),
        in_specs=[SMEM] + [VMEM] * 7,
        out_specs=VMEM,
        compiler_params=near,
        name="far",
    )(core.astype(jnp.int32)[None], queries, own, got, acc_w, stat_w, acc_p, stat_p)


def solution(mesh):
    shape = mesh.shape
    ctx = shape["ctx"]
    fine = Mesh(
        mesh.devices.reshape(shape["dp"], 2, ctx // 4, 2, shape["head"]),
        ("dp", "zh", "x", "c", "head"),
    )
    token = ("dp", "zh", "x", "c")
    return jax.shard_map(
        on_device,
        mesh=fine,
        in_specs=(
            P(token, "head"),
            P(token, "head"),
            P(token, "head"),
            P(token, None),
            P(token),
            P("dp"),
            P(token, "head", None),
            P(token, "head", None),
            P("head"),
        ),
        out_specs=P(token, "head"),
        check_vma=False,
    )
```

```python
import math

import jax
import jax.numpy as jnp
from jax import lax
from jax.experimental import pallas as pl
from jax.experimental.pallas import tpu as pltpu
from jax.sharding import Mesh, PartitionSpec as P

HD = 128
POOLS = 8
LOG2E = math.log2(math.e)
UNIT = LOG2E / math.sqrt(HD)
STRIP = 128
SWAP = [(0, 1), (1, 0)]


def dot_nt(a, b):
    return lax.dot_general(a, b, (((1,), (1,)), ((), ())), preferred_element_type=jnp.float32)


def dot_nn(a, b):
    return jnp.dot(a, b, preferred_element_type=jnp.float32)


def pool_kernel(tag_ref, seg_ref, key_ref, value_ref, out_ref, key_buf, value_buf, sems):
    rows, width = key_ref.shape
    pieces = sems.shape[1]
    step = rows // pieces
    copies = [
        [
            pltpu.make_async_copy(
                src.at[pl.ds(i * step, step)], buf.at[pl.ds(i * step, step)], sems.at[j, i]
            )
            for i in range(pieces)
        ]
        for j, (src, buf) in enumerate(((key_ref, key_buf), (value_ref, value_buf)))
    ]
    for line in copies:
        for copy in line:
            copy.start()
    seg = seg_ref[...]
    member = seg == lax.broadcasted_iota(jnp.int32, (POOLS, rows), 0)
    count = jnp.sum(member.astype(jnp.float32), axis=1, keepdims=True)
    member = member.astype(jnp.float32).astype(jnp.bfloat16)
    tag = jnp.full((POOLS, HD), tag_ref[0], jnp.int32)
    out_ref[:, 2 * width :] = tag.astype(jnp.float32).astype(jnp.bfloat16)
    for j, buf in enumerate((key_buf, value_buf)):
        for copy in copies[j]:
            copy.wait()
        mean = dot_nn(member, buf[...]) / count
        out_ref[:, j * width : (j + 1) * width] = mean.astype(jnp.bfloat16)


def soft(scores):
    top = jnp.max(scores, axis=0, keepdims=True)
    exp_terms = jnp.exp2(scores - top)
    return top, jnp.sum(exp_terms, axis=0, keepdims=True), exp_terms.astype(jnp.bfloat16)


def window_kernel(q_ref, k_ref, v_ref, acc_ref, stat_ref, buf, sems):
    copies = []
    for head in range(q_ref.shape[1] // HD):
        cols = pl.ds(head * HD, HD)
        values = v_ref[:, cols].T
        for start in range(0, q_ref.shape[0], STRIP):
            rows = pl.ds(start, STRIP)
            top, total, weights = soft(dot_nt(k_ref[:, cols], q_ref[rows, cols]) * UNIT)
            buf[cols, rows] = dot_nn(values, weights)
            stat_ref[2 * head : 2 * head + 1, rows] = top
            stat_ref[2 * head + 1 : 2 * head + 2, rows] = total
        copies.append(pltpu.make_async_copy(buf.at[cols], acc_ref.at[cols], sems.at[head]))
        copies[-1].start()
    for copy in copies:
        copy.wait()


def pooled_kernel(tag_ref, slope_ref, q_ref, p_ref, acc_ref, stat_ref, buf, sems):
    count, width = q_ref.shape
    tags = p_ref[:, 2 * width :].astype(jnp.float32)
    dist = jnp.abs(tags - tag_ref[0].astype(jnp.float32)) * LOG2E
    dist = jnp.concatenate([dist] * (count // HD), axis=1)
    copies = []
    for head in range(width // HD):
        cols = pl.ds(head * HD, HD)
        scores = dot_nt(p_ref[:, cols], q_ref[:, cols]) * UNIT - dist * slope_ref[head]
        top, total, weights = soft(scores)
        buf[cols, :] = dot_nn(p_ref[:, pl.ds(width + head * HD, HD)].T, weights)
        stat_ref[2 * head : 2 * head + 1, :] = top
        stat_ref[2 * head + 1 : 2 * head + 2, :] = total
        copies.append(pltpu.make_async_copy(buf.at[cols], acc_ref.at[cols], sems.at[head]))
        copies[-1].start()
    for copy in copies:
        copy.wait()


def ref_kernel(
    core_ref,
    q_ref,
    own_ref,
    got_ref,
    acc_w_ref,
    stat_w_ref,
    acc_p_ref,
    stat_p_ref,
    out_ref,
    buf_w,
    buf_p,
    buf_out,
    sems,
):
    first = core_ref[0] == 0
    all_cols = [pl.ds(head * HD, HD) for head in range(q_ref.shape[1] // HD)]
    fetch, store = [], []
    for head, cols in enumerate(all_cols):
        fetch.append(
            (
                pltpu.make_async_copy(acc_w_ref.at[cols], buf_w.at[cols], sems.at[0, head]),
                pltpu.make_async_copy(acc_p_ref.at[cols], buf_p.at[cols], sems.at[1, head]),
            )
        )
        for copy in fetch[-1]:
            copy.start()
    for head, cols in enumerate(all_cols):
        top_at, total_at = slice(2 * head, 2 * head + 1), slice(2 * head + 1, 2 * head + 2)
        keys = jnp.where(first, own_ref[:, cols], got_ref[:, cols])
        values = jnp.where(first, got_ref[:, cols], own_ref[:, cols]).T
        for copy in fetch[head]:
            copy.wait()
        for start in range(0, q_ref.shape[0], STRIP):
            rows = pl.ds(start, STRIP)
            top, total, weights = soft(dot_nt(keys, q_ref[rows, cols]) * UNIT)
            num = dot_nn(values, weights)
            top_w, top_p = stat_w_ref[top_at, rows], stat_p_ref[top_at, rows]
            ceiling = jnp.maximum(jnp.maximum(top_w, top_p), top)
            share_w, share_p = jnp.exp2(top_w - ceiling), jnp.exp2(top_p - ceiling)
            share = jnp.exp2(top - ceiling)
            scale = 1.0 / (
                share_w * stat_w_ref[total_at, rows]
                + share_p * stat_p_ref[total_at, rows]
                + share * total
            )
            merged = (
                (share_w * scale) * buf_w[cols, rows]
                + (share_p * scale) * buf_p[cols, rows]
                + (share * scale) * num
            )
            buf_out[rows, cols] = merged.astype(jnp.bfloat16).T
        store.append(
            pltpu.make_async_copy(buf_out.at[:, cols], out_ref.at[:, cols], sems.at[2, head])
        )
        store[-1].start()
    for copy in store:
        copy.wait()


SMEM = pl.BlockSpec(memory_space=pltpu.SMEM)
VMEM = pl.BlockSpec(memory_space=pltpu.VMEM)
HBM = pl.BlockSpec(memory_space=pltpu.HBM)
DMA = pltpu.SemaphoreType.DMA


def on_device(
    queries, keys, values, pool_segments, window_map, ref_owner, ref_keys, ref_values, slopes
):
    rows, width = queries.shape
    heads = width // HD
    n_zh, n_x, n_head = lax.axis_size("zh"), lax.axis_size("x"), lax.axis_size("head")
    ref_rows = ref_keys.shape[1]
    part = ref_rows // n_x
    core = lax.axis_index("c")
    owner = ref_owner[0]
    owner_c = owner % 2
    owner_x = (owner // 2) % n_x
    owner_z = owner // (2 * n_x)

    tie = lax.optimization_barrier
    near = pltpu.CompilerParams(vmem_limit_bytes=16 * 1024 * 1024)
    state = (
        jax.ShapeDtypeStruct((width, rows), jnp.float32),
        jax.ShapeDtypeStruct((16, rows), jnp.float32),
    )

    slot_k, slot_v = ref_keys[0], ref_values[0]
    got_k = lax.ppermute(slot_k, "c", [(1, 0)])
    got_v = lax.ppermute(slot_v, "c", [(0, 1)])
    kept = tie(jnp.where(core == 0, slot_k, slot_v))
    pooled = pl.pallas_call(
        pool_kernel,
        out_shape=jax.ShapeDtypeStruct((POOLS, 2 * width + HD), jnp.bfloat16),
        in_specs=[SMEM, VMEM, HBM, HBM],
        out_specs=VMEM,
        scratch_shapes=[
            pltpu.VMEM((rows, width), jnp.bfloat16),
            pltpu.VMEM((rows, width), jnp.bfloat16),
            DMA((2, 4)),
        ],
        compiler_params=near,
        name="pool",
    )(window_map, pool_segments, keys, values)
    mine = jnp.where(owner_c == core, kept, jnp.where(core == 0, got_k, got_v))
    mine, pooled = tie((mine, pooled))

    spread = lax.all_to_all(mine.reshape(n_x, part, -1), "x", 0, 0, tiled=True)
    other = lax.ppermute(pooled, "zh", SWAP)
    piece = lax.dynamic_index_in_dim(spread, owner_x, 0, keepdims=False)
    piece = piece.reshape(part, n_head, width).transpose(1, 0, 2)
    piece = jnp.broadcast_to(piece[None], (n_zh, n_head, part, width))
    piece, pooled, other = tie((piece, pooled, other))

    turned = lax.all_to_all(
        piece.reshape(n_zh * n_head, part, width), ("zh", "head"), 0, 0, tiled=True
    )
    pooled = jnp.concatenate([pooled, other], axis=0)
    other = lax.ppermute(pooled, "x", [(i, i ^ 1) for i in range(n_x)])
    pooled = jnp.concatenate([pooled, other], axis=0)
    other = lax.ppermute(pooled, "x", [(i, i ^ 2) for i in range(n_x)])
    turned = turned.reshape(n_zh, n_head * part, width)
    block = lax.dynamic_index_in_dim(turned, owner_z, 0, keepdims=False)
    block = jnp.broadcast_to(block[None], (n_x, n_head * part, width))
    block, pooled, other, queries_w = tie((block, pooled, other, queries))

    own = lax.all_to_all(block, "x", 0, 0, tiled=True).reshape(-1, width)
    pooled = jnp.concatenate([pooled, other], axis=0)
    other = lax.ppermute(pooled, "c", SWAP)
    scratch = [pltpu.VMEM((width, rows), jnp.float32), DMA((heads,))]
    acc_w, stat_w = pl.pallas_call(
        window_kernel,
        out_shape=state,
        in_specs=[VMEM] * 3,
        out_specs=(HBM, VMEM),
        scratch_shapes=scratch,
        compiler_params=near,
        cost_estimate=pl.CostEstimate(
            flops=4 * rows * rows * width,
            bytes_accessed=10 * rows * width,
            transcendentals=rows * rows * heads,
        ),
        name="window",
    )(queries_w, keys, values)
    pooled = jnp.concatenate([pooled, other], axis=0)
    acc_p, stat_p = pl.pallas_call(
        pooled_kernel,
        out_shape=state,
        in_specs=[SMEM, SMEM, VMEM, VMEM],
        out_specs=(HBM, VMEM),
        scratch_shapes=scratch,
        compiler_params=near,
        cost_estimate=pl.CostEstimate(
            flops=4 * rows * pooled.shape[0] * width,
            bytes_accessed=6 * rows * width,
            transcendentals=rows * pooled.shape[0] * heads,
        ),
        name="pooled",
    )(window_map, slopes, queries_w, pooled)
    own, stat_w, stat_p = tie((own, stat_w, stat_p))

    got = lax.ppermute(own, "c", SWAP)
    return pl.pallas_call(
        ref_kernel,
        out_shape=jax.ShapeDtypeStruct((rows, width), jnp.bfloat16),
        in_specs=[SMEM] + [VMEM] * 3 + [HBM, VMEM, HBM, VMEM],
        out_specs=HBM,
        scratch_shapes=[
            pltpu.VMEM((width, rows), jnp.float32),
            pltpu.VMEM((width, rows), jnp.float32),
            pltpu.VMEM((rows, width), jnp.bfloat16),
            DMA((3, heads)),
        ],
        compiler_params=near,
        name="far",
    )(core.astype(jnp.int32)[None], queries, own, got, acc_w, stat_w, acc_p, stat_p)


def solution(mesh):
    shape = mesh.shape
    ctx = shape["ctx"]
    fine = Mesh(
        mesh.devices.reshape(shape["dp"], 2, ctx // 4, 2, shape["head"]),
        ("dp", "zh", "x", "c", "head"),
    )
    token = ("dp", "zh", "x", "c")
    return jax.shard_map(
        on_device,
        mesh=fine,
        in_specs=(
            P(token, "head"),
            P(token, "head"),
            P(token, "head"),
            P(token, None),
            P(token),
            P("dp"),
            P(token, "head", None),
            P(token, "head", None),
            P("head"),
        ),
        out_specs=P(token, "head"),
        check_vma=False,
    )
```

```python
import math

import jax
import jax.numpy as jnp
from jax import lax
from jax.experimental import pallas as pl
from jax.experimental.pallas import tpu as pltpu
from jax.sharding import Mesh, PartitionSpec as P

HD = 128
POOLS = 8
LOG2E = math.log2(math.e)
UNIT = LOG2E / math.sqrt(HD)
STRIP = 128
SWAP = [(0, 1), (1, 0)]


def dot_nt(a, b):
    return lax.dot_general(a, b, (((1,), (1,)), ((), ())), preferred_element_type=jnp.float32)


def dot_nn(a, b):
    return jnp.dot(a, b, preferred_element_type=jnp.float32)


def pool_kernel(tag_ref, seg_ref, key_ref, value_ref, out_ref):
    seg = seg_ref[...]
    member = seg == lax.broadcasted_iota(jnp.int32, (POOLS, seg.shape[1]), 0)
    count = jnp.sum(member.astype(jnp.float32), axis=1, keepdims=True)
    member = member.astype(jnp.float32).astype(jnp.bfloat16)
    width = key_ref.shape[1]
    out_ref[:, :width] = (dot_nn(member, key_ref[...]) / count).astype(jnp.bfloat16)
    out_ref[:, width : 2 * width] = (dot_nn(member, value_ref[...]) / count).astype(jnp.bfloat16)
    tag = jnp.full((POOLS, HD), tag_ref[0], jnp.int32)
    out_ref[:, 2 * width :] = tag.astype(jnp.float32).astype(jnp.bfloat16)


def soft(scores):
    top = jnp.max(scores, axis=0, keepdims=True)
    exp_terms = jnp.exp2(scores - top)
    return top, jnp.sum(exp_terms, axis=0, keepdims=True), exp_terms.astype(jnp.bfloat16)


def window_kernel(q_ref, k_ref, v_ref, acc_ref, stat_ref):
    for head in range(q_ref.shape[1] // HD):
        cols = pl.ds(head * HD, HD)
        values = v_ref[:, cols].T
        for start in range(0, q_ref.shape[0], STRIP):
            rows = pl.ds(start, STRIP)
            top, total, weights = soft(dot_nt(k_ref[:, cols], q_ref[rows, cols]) * UNIT)
            acc_ref[cols, rows] = dot_nn(values, weights)
            stat_ref[2 * head : 2 * head + 1, rows] = top
            stat_ref[2 * head + 1 : 2 * head + 2, rows] = total


def pooled_kernel(
    tag_ref, slope_ref, q_ref, p_ref, acc_ref, stat_ref, acc_out_ref, stat_out_ref
):
    count, width = q_ref.shape
    tags = p_ref[:, 2 * width :].astype(jnp.float32)
    dist = jnp.abs(tags - tag_ref[0].astype(jnp.float32)) * LOG2E
    dist = jnp.concatenate([dist] * (count // HD), axis=1)
    for head in range(width // HD):
        cols = pl.ds(head * HD, HD)
        scores = dot_nt(p_ref[:, cols], q_ref[:, cols]) * UNIT - dist * slope_ref[head]
        top, total, weights = soft(scores)
        num = dot_nn(p_ref[:, pl.ds(width + head * HD, HD)].T, weights)
        top_n = stat_ref[2 * head : 2 * head + 1, :]
        total_n = stat_ref[2 * head + 1 : 2 * head + 2, :]
        ceiling = jnp.maximum(top_n, top)
        share_n, share = jnp.exp2(top_n - ceiling), jnp.exp2(top - ceiling)
        acc_out_ref[cols, :] = share_n * acc_ref[cols, :] + share * num
        stat_out_ref[2 * head : 2 * head + 1, :] = ceiling
        stat_out_ref[2 * head + 1 : 2 * head + 2, :] = share_n * total_n + share * total


def ref_kernel(core_ref, q_ref, own_ref, got_ref, acc_ref, stat_ref, out_ref):
    first = core_ref[0] == 0
    for head in range(q_ref.shape[1] // HD):
        cols = pl.ds(head * HD, HD)
        keys = jnp.where(first, own_ref[:, cols], got_ref[:, cols])
        values = jnp.where(first, got_ref[:, cols], own_ref[:, cols]).T
        for start in range(0, q_ref.shape[0], STRIP):
            rows = pl.ds(start, STRIP)
            top, total, weights = soft(dot_nt(keys, q_ref[rows, cols]) * UNIT)
            num = dot_nn(values, weights)
            top_n = stat_ref[2 * head : 2 * head + 1, rows]
            total_n = stat_ref[2 * head + 1 : 2 * head + 2, rows]
            ceiling = jnp.maximum(top_n, top)
            share_n, share = jnp.exp2(top_n - ceiling), jnp.exp2(top - ceiling)
            scale = 1.0 / (share_n * total_n + share * total)
            merged = (share_n * scale) * acc_ref[cols, rows] + (share * scale) * num
            out_ref[rows, cols] = merged.astype(jnp.bfloat16).T


SMEM = pl.BlockSpec(memory_space=pltpu.SMEM)
VMEM = pl.BlockSpec(memory_space=pltpu.VMEM)


def on_device(
    queries, keys, values, pool_segments, window_map, ref_owner, ref_keys, ref_values, slopes
):
    rows, width = queries.shape
    heads = width // HD
    n_zh, n_x, n_head = lax.axis_size("zh"), lax.axis_size("x"), lax.axis_size("head")
    ref_rows = ref_keys.shape[1]
    part = ref_rows // n_x
    core = lax.axis_index("c")
    owner = ref_owner[0]
    owner_c = owner % 2
    owner_x = (owner // 2) % n_x
    owner_z = owner // (2 * n_x)

    tie = lax.optimization_barrier
    near = pltpu.CompilerParams(vmem_limit_bytes=10 * 1024 * 1024)
    state = (
        jax.ShapeDtypeStruct((width, rows), jnp.float32),
        jax.ShapeDtypeStruct((16, rows), jnp.float32),
    )

    slot_k, slot_v = ref_keys[0], ref_values[0]
    got_k = lax.ppermute(slot_k, "c", [(1, 0)])
    got_v = lax.ppermute(slot_v, "c", [(0, 1)])
    kept = tie(jnp.where(core == 0, slot_k, slot_v))
    pooled = pl.pallas_call(
        pool_kernel,
        out_shape=jax.ShapeDtypeStruct((POOLS, 2 * width + HD), jnp.bfloat16),
        in_specs=[SMEM, VMEM, VMEM, VMEM],
        out_specs=VMEM,
        compiler_params=near,
        name="pool",
    )(window_map, pool_segments, keys, values)
    mine = jnp.where(owner_c == core, kept, jnp.where(core == 0, got_k, got_v))
    mine, pooled, queries_w = tie((mine, pooled, queries))

    spread = lax.all_to_all(mine.reshape(n_x, part, -1), "x", 0, 0, tiled=True)
    other = lax.ppermute(pooled, "zh", SWAP)
    acc_w, stat_w = pl.pallas_call(
        window_kernel,
        out_shape=state,
        in_specs=[VMEM] * 3,
        out_specs=(VMEM, VMEM),
        compiler_params=near,
        cost_estimate=pl.CostEstimate(
            flops=4 * rows * rows * width,
            bytes_accessed=10 * rows * width,
            transcendentals=rows * rows * heads,
        ),
        name="window",
    )(queries_w, keys, values)
    other, stat_w = tie((other, stat_w))
    pooled = jnp.concatenate([pooled, other], axis=0)
    other = lax.ppermute(pooled, "x", [(i, i ^ 1) for i in range(n_x)])
    piece = lax.dynamic_index_in_dim(spread, owner_x, 0, keepdims=False)
    piece = piece.reshape(part, n_head, width).transpose(1, 0, 2)
    piece = jnp.broadcast_to(piece[None], (n_zh, n_head, part, width))
    piece, pooled, other = tie((piece, pooled, other))

    turned = lax.all_to_all(
        piece.reshape(n_zh * n_head, part, width), ("zh", "head"), 0, 0, tiled=True
    )
    pooled = jnp.concatenate([pooled, other], axis=0)
    other = lax.ppermute(pooled, "x", [(i, i ^ 2) for i in range(n_x)])
    turned = turned.reshape(n_zh, n_head * part, width)
    block = lax.dynamic_index_in_dim(turned, owner_z, 0, keepdims=False)
    block = jnp.broadcast_to(block[None], (n_x, n_head * part, width))
    block, pooled, other = tie((block, pooled, other))

    own = lax.all_to_all(block, "x", 0, 0, tiled=True).reshape(-1, width)
    pooled = jnp.concatenate([pooled, other], axis=0)
    other = lax.ppermute(pooled, "c", SWAP)
    pooled = jnp.concatenate([pooled, other], axis=0)
    acc, stat = pl.pallas_call(
        pooled_kernel,
        out_shape=state,
        in_specs=[SMEM, SMEM] + [VMEM] * 4,
        out_specs=(VMEM, VMEM),
        compiler_params=near,
        cost_estimate=pl.CostEstimate(
            flops=4 * rows * pooled.shape[0] * width,
            bytes_accessed=12 * rows * width,
            transcendentals=rows * pooled.shape[0] * heads,
        ),
        name="pooled",
    )(window_map, slopes, queries, pooled, acc_w, stat_w)
    own, stat = tie((own, stat))

    got = lax.ppermute(own, "c", SWAP)
    return pl.pallas_call(
        ref_kernel,
        out_shape=jax.ShapeDtypeStruct((rows, width), jnp.bfloat16),
        in_specs=[SMEM] + [VMEM] * 5,
        out_specs=VMEM,
        compiler_params=near,
        name="far",
    )(core.astype(jnp.int32)[None], queries, own, got, acc, stat)


def solution(mesh):
    shape = mesh.shape
    ctx = shape["ctx"]
    fine = Mesh(
        mesh.devices.reshape(shape["dp"], 2, ctx // 4, 2, shape["head"]),
        ("dp", "zh", "x", "c", "head"),
    )
    token = ("dp", "zh", "x", "c")
    return jax.shard_map(
        on_device,
        mesh=fine,
        in_specs=(
            P(token, "head"),
            P(token, "head"),
            P(token, "head"),
            P(token, None),
            P(token),
            P("dp"),
            P(token, "head", None),
            P(token, "head", None),
            P("head"),
        ),
        out_specs=P(token, "head"),
        check_vma=False,
    )
```

```python
import math

import jax
import jax.numpy as jnp
from jax import lax
from jax.experimental import pallas as pl
from jax.experimental.pallas import tpu as pltpu
from jax.sharding import Mesh, PartitionSpec as P

HD = 128
POOLS = 8
LOG2E = math.log2(math.e)
UNIT = LOG2E / math.sqrt(HD)
STRIP = 128
SWAP = [(0, 1), (1, 0)]


def dot_nt(a, b):
    return lax.dot_general(a, b, (((1,), (1,)), ((), ())), preferred_element_type=jnp.float32)


def dot_nn(a, b):
    return jnp.dot(a, b, preferred_element_type=jnp.float32)


def pool_kernel(seg_ref, token_ref, out_ref):
    seg = seg_ref[...]
    member = seg == lax.broadcasted_iota(jnp.int32, (POOLS, seg.shape[1]), 0)
    count = jnp.sum(member.astype(jnp.float32), axis=1, keepdims=True)
    member = member.astype(jnp.float32).astype(jnp.bfloat16)
    out_ref[...] = (dot_nn(member, token_ref[...]) / count).astype(jnp.bfloat16)


def soft(scores):
    top = jnp.max(scores, axis=0, keepdims=True)
    exp_terms = jnp.exp2(scores - top)
    return top, jnp.sum(exp_terms, axis=0, keepdims=True), exp_terms.astype(jnp.bfloat16)


def window_kernel(q_ref, k_ref, v_ref, acc_ref, stat_ref):
    for head in range(q_ref.shape[1] // HD):
        cols = pl.ds(head * HD, HD)
        values = v_ref[:, cols].T
        for start in range(0, q_ref.shape[0], STRIP):
            rows = pl.ds(start, STRIP)
            top, total, weights = soft(dot_nt(k_ref[:, cols], q_ref[rows, cols]) * UNIT)
            acc_ref[cols, rows] = dot_nn(values, weights)
            stat_ref[2 * head : 2 * head + 1, rows] = top
            stat_ref[2 * head + 1 : 2 * head + 2, rows] = total


def pooled_kernel(
    tag_ref, slope_ref, q_ref, p_ref, acc_ref, stat_ref, acc_out_ref, stat_out_ref
):
    count, width = q_ref.shape
    tags = p_ref[:, 2 * width :].astype(jnp.float32)
    dist = jnp.abs(tags - tag_ref[0].astype(jnp.float32)) * LOG2E
    dist = jnp.concatenate([dist] * (count // HD), axis=1)
    for head in range(width // HD):
        cols = pl.ds(head * HD, HD)
        scores = dot_nt(p_ref[:, cols], q_ref[:, cols]) * UNIT - dist * slope_ref[head]
        top, total, weights = soft(scores)
        num = dot_nn(p_ref[:, pl.ds(width + head * HD, HD)].T, weights)
        top_n = stat_ref[2 * head : 2 * head + 1, :]
        total_n = stat_ref[2 * head + 1 : 2 * head + 2, :]
        ceiling = jnp.maximum(top_n, top)
        share_n, share = jnp.exp2(top_n - ceiling), jnp.exp2(top - ceiling)
        acc_out_ref[cols, :] = share_n * acc_ref[cols, :] + share * num
        stat_out_ref[2 * head : 2 * head + 1, :] = ceiling
        stat_out_ref[2 * head + 1 : 2 * head + 2, :] = share_n * total_n + share * total


def ref_kernel(core_ref, q_ref, own_ref, got_ref, acc_ref, stat_ref, out_ref):
    first = core_ref[0] == 0
    for head in range(q_ref.shape[1] // HD):
        cols = pl.ds(head * HD, HD)
        keys = jnp.where(first, own_ref[:, cols], got_ref[:, cols])
        values = jnp.where(first, got_ref[:, cols], own_ref[:, cols]).T
        for start in range(0, q_ref.shape[0], STRIP):
            rows = pl.ds(start, STRIP)
            top, total, weights = soft(dot_nt(keys, q_ref[rows, cols]) * UNIT)
            num = dot_nn(values, weights)
            top_n = stat_ref[2 * head : 2 * head + 1, rows]
            total_n = stat_ref[2 * head + 1 : 2 * head + 2, rows]
            ceiling = jnp.maximum(top_n, top)
            share_n, share = jnp.exp2(top_n - ceiling), jnp.exp2(top - ceiling)
            scale = 1.0 / (share_n * total_n + share * total)
            merged = (share_n * scale) * acc_ref[cols, rows] + (share * scale) * num
            out_ref[rows, cols] = merged.astype(jnp.bfloat16).T


SMEM = pl.BlockSpec(memory_space=pltpu.SMEM)
VMEM = pl.BlockSpec(memory_space=pltpu.VMEM)


def on_device(
    queries, keys, values, pool_segments, window_map, ref_owner, ref_keys, ref_values, slopes
):
    rows, width = queries.shape
    heads = width // HD
    n_zh, n_x, n_head = lax.axis_size("zh"), lax.axis_size("x"), lax.axis_size("head")
    ref_rows = ref_keys.shape[1]
    part = ref_rows // n_x
    core = lax.axis_index("c")
    owner = ref_owner[0]
    owner_c = owner % 2
    owner_x = (owner // 2) % n_x
    owner_z = owner // (2 * n_x)

    tie = lax.optimization_barrier
    near = pltpu.CompilerParams(vmem_limit_bytes=10 * 1024 * 1024)
    state = (
        jax.ShapeDtypeStruct((width, rows), jnp.float32),
        jax.ShapeDtypeStruct((16, rows), jnp.float32),
    )

    slot_k, slot_v = ref_keys[0], ref_values[0]
    got_k = lax.ppermute(slot_k, "c", [(1, 0)])
    got_v = lax.ppermute(slot_v, "c", [(0, 1)])
    kept = tie(jnp.where(core == 0, slot_k, slot_v))
    pool = pl.pallas_call(
        pool_kernel,
        out_shape=jax.ShapeDtypeStruct((POOLS, width), jnp.bfloat16),
        in_specs=[VMEM, VMEM],
        out_specs=VMEM,
        compiler_params=near,
        name="pool",
    )
    pooled_k = pool(pool_segments, keys)
    pooled_k, values_p = tie((pooled_k, values))
    pooled_v = pool(pool_segments, values_p)
    tag = jnp.broadcast_to(window_map.astype(jnp.bfloat16)[:, None], (POOLS, HD))
    pooled = jnp.concatenate([pooled_k, pooled_v, tag], axis=1)
    mine = jnp.where(owner_c == core, kept, jnp.where(core == 0, got_k, got_v))
    mine, pooled = tie((mine, pooled))

    spread = lax.all_to_all(mine.reshape(n_x, part, -1), "x", 0, 0, tiled=True)
    other = lax.ppermute(pooled, "x", [(i, i ^ 1) for i in range(n_x)])
    pooled = jnp.concatenate([pooled, other], axis=0)
    other = lax.ppermute(pooled, "zh", SWAP)
    piece = lax.dynamic_index_in_dim(spread, owner_x, 0, keepdims=False)
    piece = piece.reshape(part, n_head, width).transpose(1, 0, 2)
    piece = jnp.broadcast_to(piece[None], (n_zh, n_head, part, width))
    piece, pooled, other, queries_w = tie((piece, pooled, other, queries))

    turned = lax.all_to_all(
        piece.reshape(n_zh * n_head, part, width), ("zh", "head"), 0, 0, tiled=True
    )
    pooled = jnp.concatenate([pooled, other], axis=0)
    other = lax.ppermute(pooled, "x", [(i, i ^ 2) for i in range(n_x)])
    acc_w, stat_w = pl.pallas_call(
        window_kernel,
        out_shape=state,
        in_specs=[VMEM] * 3,
        out_specs=(VMEM, VMEM),
        compiler_params=near,
        cost_estimate=pl.CostEstimate(
            flops=4 * rows * rows * width,
            bytes_accessed=10 * rows * width,
            transcendentals=rows * rows * heads,
        ),
        name="window",
    )(queries_w, keys, values)
    turned = turned.reshape(n_zh, n_head * part, width)
    block = lax.dynamic_index_in_dim(turned, owner_z, 0, keepdims=False)
    block = jnp.broadcast_to(block[None], (n_x, n_head * part, width))
    block, pooled, other, stat_w = tie((block, pooled, other, stat_w))

    own = lax.all_to_all(block, "x", 0, 0, tiled=True).reshape(-1, width)
    pooled = jnp.concatenate([pooled, other], axis=0)
    other = lax.ppermute(pooled, "c", SWAP)
    pooled = jnp.concatenate([pooled, other], axis=0)
    acc, stat = pl.pallas_call(
        pooled_kernel,
        out_shape=state,
        in_specs=[SMEM, SMEM] + [VMEM] * 4,
        out_specs=(VMEM, VMEM),
        compiler_params=near,
        cost_estimate=pl.CostEstimate(
            flops=4 * rows * pooled.shape[0] * width,
            bytes_accessed=12 * rows * width,
            transcendentals=rows * pooled.shape[0] * heads,
        ),
        name="pooled",
    )(window_map, slopes, queries, pooled, acc_w, stat_w)
    own, stat = tie((own, stat))

    got = lax.ppermute(own, "c", SWAP)
    return pl.pallas_call(
        ref_kernel,
        out_shape=jax.ShapeDtypeStruct((rows, width), jnp.bfloat16),
        in_specs=[SMEM] + [VMEM] * 5,
        out_specs=VMEM,
        compiler_params=near,
        name="far",
    )(core.astype(jnp.int32)[None], queries, own, got, acc, stat)


def solution(mesh):
    shape = mesh.shape
    ctx = shape["ctx"]
    fine = Mesh(
        mesh.devices.reshape(shape["dp"], 2, ctx // 4, 2, shape["head"]),
        ("dp", "zh", "x", "c", "head"),
    )
    token = ("dp", "zh", "x", "c")
    return jax.shard_map(
        on_device,
        mesh=fine,
        in_specs=(
            P(token, "head"),
            P(token, "head"),
            P(token, "head"),
            P(token, None),
            P(token),
            P("dp"),
            P(token, "head", None),
            P(token, "head", None),
            P("head"),
        ),
        out_specs=P(token, "head"),
        check_vma=False,
    )
```

```python
import math

import jax
import jax.numpy as jnp
from jax import lax
from jax.experimental import pallas as pl
from jax.experimental.pallas import tpu as pltpu
from jax.sharding import Mesh, PartitionSpec as P

HD = 128
POOLS = 8
LOG2E = math.log2(math.e)
UNIT = LOG2E / math.sqrt(HD)
STRIP = 128
SWAP = [(0, 1), (1, 0)]


def dot_nt(a, b):
    return lax.dot_general(a, b, (((1,), (1,)), ((), ())), preferred_element_type=jnp.float32)


def dot_nn(a, b):
    return jnp.dot(a, b, preferred_element_type=jnp.float32)


def pool_kernel(tag_ref, seg_ref, key_ref, value_ref, out_ref):
    seg = seg_ref[...]
    member = seg == lax.broadcasted_iota(jnp.int32, (POOLS, seg.shape[1]), 0)
    count = jnp.sum(member.astype(jnp.float32), axis=1, keepdims=True)
    member = member.astype(jnp.float32).astype(jnp.bfloat16)
    width = key_ref.shape[1]
    out_ref[:, :width] = (dot_nn(member, key_ref[...]) / count).astype(jnp.bfloat16)
    out_ref[:, width : 2 * width] = (dot_nn(member, value_ref[...]) / count).astype(jnp.bfloat16)
    tag = jnp.full((POOLS, HD), tag_ref[0], jnp.int32)
    out_ref[:, 2 * width :] = tag.astype(jnp.float32).astype(jnp.bfloat16)


def soft(scores):
    top = jnp.max(scores, axis=0, keepdims=True)
    exp_terms = jnp.exp2(scores - top)
    return top, jnp.sum(exp_terms, axis=0, keepdims=True), exp_terms.astype(jnp.bfloat16)


def window_kernel(q_ref, k_ref, v_ref, acc_ref, stat_ref):
    for head in range(q_ref.shape[1] // HD):
        cols = pl.ds(head * HD, HD)
        values = v_ref[:, cols].T
        for start in range(0, q_ref.shape[0], STRIP):
            rows = pl.ds(start, STRIP)
            top, total, weights = soft(dot_nt(k_ref[:, cols], q_ref[rows, cols]) * UNIT)
            acc_ref[cols, rows] = dot_nn(values, weights)
            stat_ref[2 * head : 2 * head + 1, rows] = top
            stat_ref[2 * head + 1 : 2 * head + 2, rows] = total


def pooled_kernel(
    tag_ref, slope_ref, q_ref, p_ref, acc_ref, stat_ref, acc_out_ref, stat_out_ref
):
    count, width = q_ref.shape
    tags = p_ref[:, 2 * width :].astype(jnp.float32)
    dist = jnp.abs(tags - tag_ref[0].astype(jnp.float32)) * LOG2E
    dist = jnp.concatenate([dist] * (count // HD), axis=1)
    for head in range(width // HD):
        cols = pl.ds(head * HD, HD)
        scores = dot_nt(p_ref[:, cols], q_ref[:, cols]) * UNIT - dist * slope_ref[head]
        top, total, weights = soft(scores)
        num = dot_nn(p_ref[:, pl.ds(width + head * HD, HD)].T, weights)
        top_n = stat_ref[2 * head : 2 * head + 1, :]
        total_n = stat_ref[2 * head + 1 : 2 * head + 2, :]
        ceiling = jnp.maximum(top_n, top)
        share_n, share = jnp.exp2(top_n - ceiling), jnp.exp2(top - ceiling)
        acc_out_ref[cols, :] = share_n * acc_ref[cols, :] + share * num
        stat_out_ref[2 * head : 2 * head + 1, :] = ceiling
        stat_out_ref[2 * head + 1 : 2 * head + 2, :] = share_n * total_n + share * total


def ref_kernel(core_ref, q_ref, own_ref, got_ref, acc_ref, stat_ref, out_ref):
    first = core_ref[0] == 0
    for head in range(q_ref.shape[1] // HD):
        cols = pl.ds(head * HD, HD)
        keys = jnp.where(first, own_ref[:, cols], got_ref[:, cols])
        values = jnp.where(first, got_ref[:, cols], own_ref[:, cols]).T
        for start in range(0, q_ref.shape[0], STRIP):
            rows = pl.ds(start, STRIP)
            top, total, weights = soft(dot_nt(keys, q_ref[rows, cols]) * UNIT)
            num = dot_nn(values, weights)
            top_n = stat_ref[2 * head : 2 * head + 1, rows]
            total_n = stat_ref[2 * head + 1 : 2 * head + 2, rows]
            ceiling = jnp.maximum(top_n, top)
            share_n, share = jnp.exp2(top_n - ceiling), jnp.exp2(top - ceiling)
            scale = 1.0 / (share_n * total_n + share * total)
            merged = (share_n * scale) * acc_ref[cols, rows] + (share * scale) * num
            out_ref[rows, cols] = merged.astype(jnp.bfloat16).T


SMEM = pl.BlockSpec(memory_space=pltpu.SMEM)
VMEM = pl.BlockSpec(memory_space=pltpu.VMEM)


def on_device(
    queries, keys, values, pool_segments, window_map, ref_owner, ref_keys, ref_values, slopes
):
    rows, width = queries.shape
    heads = width // HD
    n_zh, n_x, n_head = lax.axis_size("zh"), lax.axis_size("x"), lax.axis_size("head")
    ref_rows = ref_keys.shape[1]
    part = ref_rows // n_x
    core = lax.axis_index("c")
    owner = ref_owner[0]
    owner_c = owner % 2
    owner_x = (owner // 2) % n_x
    owner_z = owner // (2 * n_x)

    tie = lax.optimization_barrier
    near = pltpu.CompilerParams(vmem_limit_bytes=10 * 1024 * 1024)
    state = (
        jax.ShapeDtypeStruct((width, rows), jnp.float32),
        jax.ShapeDtypeStruct((16, rows), jnp.float32),
    )

    slot_k, slot_v = ref_keys[0], ref_values[0]
    got_k = lax.ppermute(slot_k, "c", [(1, 0)])
    got_v = lax.ppermute(slot_v, "c", [(0, 1)])
    kept = tie(jnp.where(core == 0, slot_k, slot_v))
    pooled = pl.pallas_call(
        pool_kernel,
        out_shape=jax.ShapeDtypeStruct((POOLS, 2 * width + HD), jnp.bfloat16),
        in_specs=[SMEM, VMEM, VMEM, VMEM],
        out_specs=VMEM,
        compiler_params=near,
        name="pool",
    )(window_map, pool_segments, keys, values)
    mine = jnp.where(owner_c == core, kept, jnp.where(core == 0, got_k, got_v))
    mine, pooled = tie((mine, pooled))

    spread = lax.all_to_all(mine.reshape(n_x, part, -1), "x", 0, 0, tiled=True)
    other = lax.ppermute(pooled, "zh", SWAP)
    piece = lax.dynamic_index_in_dim(spread, owner_x, 0, keepdims=False)
    piece = piece.reshape(part, n_head, width).transpose(1, 0, 2)
    piece = jnp.broadcast_to(piece[None], (n_zh, n_head, part, width))
    piece, pooled, other, queries_w = tie((piece, pooled, other, queries))

    turned = lax.all_to_all(
        piece.reshape(n_zh * n_head, part, width), ("zh", "head"), 0, 0, tiled=True
    )
    pooled = jnp.concatenate([pooled, other], axis=0)
    other = lax.ppermute(pooled, "x", [(i, i ^ 1) for i in range(n_x)])
    acc_w, stat_w = pl.pallas_call(
        window_kernel,
        out_shape=state,
        in_specs=[VMEM] * 3,
        out_specs=(VMEM, VMEM),
        compiler_params=near,
        cost_estimate=pl.CostEstimate(
            flops=4 * rows * rows * width,
            bytes_accessed=10 * rows * width,
            transcendentals=rows * rows * heads,
        ),
        name="window",
    )(queries_w, keys, values)
    other, stat_w = tie((other, stat_w))
    pooled = jnp.concatenate([pooled, other], axis=0)
    turned = turned.reshape(n_zh, n_head * part, width)
    block = lax.dynamic_index_in_dim(turned, owner_z, 0, keepdims=False)
    block = jnp.broadcast_to(block[None], (n_x, n_head * part, width))
    other = lax.ppermute(pooled, "x", [(i, i ^ 2) for i in range(n_x)])

    own = lax.all_to_all(block, "x", 0, 0, tiled=True).reshape(-1, width)
    pooled = jnp.concatenate([pooled, other], axis=0)
    other = lax.ppermute(pooled, "c", SWAP)
    pooled = jnp.concatenate([pooled, other], axis=0)
    acc, stat = pl.pallas_call(
        pooled_kernel,
        out_shape=state,
        in_specs=[SMEM, SMEM] + [VMEM] * 4,
        out_specs=(VMEM, VMEM),
        compiler_params=near,
        cost_estimate=pl.CostEstimate(
            flops=4 * rows * pooled.shape[0] * width,
            bytes_accessed=12 * rows * width,
            transcendentals=rows * pooled.shape[0] * heads,
        ),
        name="pooled",
    )(window_map, slopes, queries, pooled, acc_w, stat_w)
    own, stat = tie((own, stat))

    got = lax.ppermute(own, "c", SWAP)
    return pl.pallas_call(
        ref_kernel,
        out_shape=jax.ShapeDtypeStruct((rows, width), jnp.bfloat16),
        in_specs=[SMEM] + [VMEM] * 5,
        out_specs=VMEM,
        compiler_params=near,
        name="far",
    )(core.astype(jnp.int32)[None], queries, own, got, acc, stat)


def solution(mesh):
    shape = mesh.shape
    ctx = shape["ctx"]
    fine = Mesh(
        mesh.devices.reshape(shape["dp"], 2, ctx // 4, 2, shape["head"]),
        ("dp", "zh", "x", "c", "head"),
    )
    token = ("dp", "zh", "x", "c")
    return jax.shard_map(
        on_device,
        mesh=fine,
        in_specs=(
            P(token, "head"),
            P(token, "head"),
            P(token, "head"),
            P(token, None),
            P(token),
            P("dp"),
            P(token, "head", None),
            P(token, "head", None),
            P("head"),
        ),
        out_specs=P(token, "head"),
        check_vma=False,
    )
```

```python
import math

import jax
import jax.numpy as jnp
from jax import lax
from jax.experimental import pallas as pl
from jax.experimental.pallas import tpu as pltpu
from jax.sharding import Mesh, PartitionSpec as P

HD = 128
POOLS = 8
LOG2E = math.log2(math.e)
UNIT = LOG2E / math.sqrt(HD)
STRIP = 128
SWAP = [(0, 1), (1, 0)]


def dot_nt(a, b):
    return lax.dot_general(a, b, (((1,), (1,)), ((), ())), preferred_element_type=jnp.float32)


def dot_nn(a, b):
    return jnp.dot(a, b, preferred_element_type=jnp.float32)


def pool_kernel(tag_ref, seg_ref, key_ref, value_ref, out_ref):
    seg = seg_ref[...]
    member = seg == lax.broadcasted_iota(jnp.int32, (POOLS, seg.shape[1]), 0)
    count = jnp.sum(member.astype(jnp.float32), axis=1, keepdims=True)
    member = member.astype(jnp.float32).astype(jnp.bfloat16)
    width = key_ref.shape[1]
    out_ref[:, :width] = (dot_nn(member, key_ref[...]) / count).astype(jnp.bfloat16)
    out_ref[:, width : 2 * width] = (dot_nn(member, value_ref[...]) / count).astype(jnp.bfloat16)
    tag = jnp.full((POOLS, HD), tag_ref[0], jnp.int32)
    out_ref[:, 2 * width :] = tag.astype(jnp.float32).astype(jnp.bfloat16)


def soft(scores):
    top = jnp.max(scores, axis=0, keepdims=True)
    exp_terms = jnp.exp2(scores - top)
    return top, jnp.sum(exp_terms, axis=0, keepdims=True), exp_terms.astype(jnp.bfloat16)


def window_kernel(q_ref, k_ref, v_ref, acc_ref, stat_ref):
    for head in range(q_ref.shape[1] // HD):
        cols = pl.ds(head * HD, HD)
        values = v_ref[:, cols].T
        for start in range(0, q_ref.shape[0], STRIP):
            rows = pl.ds(start, STRIP)
            top, total, weights = soft(dot_nt(k_ref[:, cols], q_ref[rows, cols]) * UNIT)
            acc_ref[cols, rows] = dot_nn(values, weights)
            stat_ref[2 * head : 2 * head + 1, rows] = top
            stat_ref[2 * head + 1 : 2 * head + 2, rows] = total


def pooled_kernel(
    tag_ref, slope_ref, q_ref, pa_ref, pb_ref, acc_ref, stat_ref, acc_out_ref, stat_out_ref
):
    count, width = q_ref.shape

    def both(first):
        cols = pl.ds(first, HD)
        return jnp.concatenate([pa_ref[:, cols], pb_ref[:, cols]], axis=0)

    tags = both(2 * width).astype(jnp.float32)
    dist = jnp.abs(tags - tag_ref[0].astype(jnp.float32)) * LOG2E
    dist = jnp.concatenate([dist] * (count // HD), axis=1)
    for head in range(width // HD):
        cols = pl.ds(head * HD, HD)
        scores = dot_nt(both(head * HD), q_ref[:, cols]) * UNIT - dist * slope_ref[head]
        top, total, weights = soft(scores)
        num = dot_nn(both(width + head * HD).T, weights)
        top_n = stat_ref[2 * head : 2 * head + 1, :]
        total_n = stat_ref[2 * head + 1 : 2 * head + 2, :]
        ceiling = jnp.maximum(top_n, top)
        share_n, share = jnp.exp2(top_n - ceiling), jnp.exp2(top - ceiling)
        acc_out_ref[cols, :] = share_n * acc_ref[cols, :] + share * num
        stat_out_ref[2 * head : 2 * head + 1, :] = ceiling
        stat_out_ref[2 * head + 1 : 2 * head + 2, :] = share_n * total_n + share * total


def ref_kernel(core_ref, q_ref, own_ref, got_ref, acc_ref, stat_ref, out_ref):
    first = core_ref[0] == 0
    for head in range(q_ref.shape[1] // HD):
        cols = pl.ds(head * HD, HD)
        keys = jnp.where(first, own_ref[:, cols], got_ref[:, cols])
        values = jnp.where(first, got_ref[:, cols], own_ref[:, cols]).T
        for start in range(0, q_ref.shape[0], STRIP):
            rows = pl.ds(start, STRIP)
            top, total, weights = soft(dot_nt(keys, q_ref[rows, cols]) * UNIT)
            num = dot_nn(values, weights)
            top_n = stat_ref[2 * head : 2 * head + 1, rows]
            total_n = stat_ref[2 * head + 1 : 2 * head + 2, rows]
            ceiling = jnp.maximum(top_n, top)
            share_n, share = jnp.exp2(top_n - ceiling), jnp.exp2(top - ceiling)
            scale = 1.0 / (share_n * total_n + share * total)
            merged = (share_n * scale) * acc_ref[cols, rows] + (share * scale) * num
            out_ref[rows, cols] = merged.astype(jnp.bfloat16).T


SMEM = pl.BlockSpec(memory_space=pltpu.SMEM)
VMEM = pl.BlockSpec(memory_space=pltpu.VMEM)


def on_device(
    queries, keys, values, pool_segments, window_map, ref_owner, ref_keys, ref_values, slopes
):
    rows, width = queries.shape
    heads = width // HD
    n_zh, n_x, n_head = lax.axis_size("zh"), lax.axis_size("x"), lax.axis_size("head")
    ref_rows = ref_keys.shape[1]
    part = ref_rows // n_x
    core = lax.axis_index("c")
    owner = ref_owner[0]
    owner_c = owner % 2
    owner_x = (owner // 2) % n_x
    owner_z = owner // (2 * n_x)

    tie = lax.optimization_barrier
    near = pltpu.CompilerParams(vmem_limit_bytes=10 * 1024 * 1024)
    state = (
        jax.ShapeDtypeStruct((width, rows), jnp.float32),
        jax.ShapeDtypeStruct((16, rows), jnp.float32),
    )

    slot_k, slot_v = ref_keys[0], ref_values[0]
    given = jnp.where(core == 0, slot_v, slot_k)
    given, slot_k, slot_v, keys_p, values_p = tie((given, slot_k, slot_v, keys, values))
    got = lax.ppermute(given, "c", SWAP)
    kept = tie(jnp.where(core == 0, slot_k, slot_v))
    pooled = pl.pallas_call(
        pool_kernel,
        out_shape=jax.ShapeDtypeStruct((POOLS, 2 * width + HD), jnp.bfloat16),
        in_specs=[SMEM, VMEM, VMEM, VMEM],
        out_specs=VMEM,
        compiler_params=near,
        name="pool",
    )(window_map, pool_segments, keys, values)
    mine = jnp.where(owner_c == core, kept, got)
    mine, pooled = tie((mine, pooled))

    spread = lax.all_to_all(mine.reshape(n_x, part, -1), "x", 0, 0, tiled=True)
    other = lax.ppermute(pooled, "zh", SWAP)
    piece = lax.dynamic_index_in_dim(spread, owner_x, 0, keepdims=False)
    piece = piece.reshape(part, n_head, width).transpose(1, 0, 2)
    piece = jnp.broadcast_to(piece[None], (n_zh, n_head, part, width))
    piece, pooled, other = tie((piece, pooled, other))

    turned = lax.all_to_all(
        piece.reshape(n_zh * n_head, part, width), ("zh", "head"), 0, 0, tiled=True
    )
    pooled = jnp.concatenate([pooled, other], axis=0)
    other = lax.ppermute(pooled, "x", [(i, i ^ 1) for i in range(n_x)])
    pooled = jnp.concatenate([pooled, other], axis=0)
    turned = turned.reshape(n_zh, n_head * part, width)
    block = lax.dynamic_index_in_dim(turned, owner_z, 0, keepdims=False)
    block = jnp.broadcast_to(block[None], (n_x, n_head * part, width))
    other = lax.ppermute(pooled, "x", [(i, i ^ 2) for i in range(n_x)])

    block, queries_w = tie((block, queries))

    own = lax.all_to_all(block, "x", 0, 0, tiled=True).reshape(-1, width)
    pooled = jnp.concatenate([pooled, other], axis=0)
    other = lax.ppermute(pooled, "c", SWAP)
    acc_w, stat_w = pl.pallas_call(
        window_kernel,
        out_shape=state,
        in_specs=[VMEM] * 3,
        out_specs=(VMEM, VMEM),
        compiler_params=near,
        cost_estimate=pl.CostEstimate(
            flops=4 * rows * rows * width,
            bytes_accessed=10 * rows * width,
            transcendentals=rows * rows * heads,
        ),
        name="window",
    )(queries_w, keys, values)
    acc, stat = pl.pallas_call(
        pooled_kernel,
        out_shape=state,
        in_specs=[SMEM, SMEM] + [VMEM] * 5,
        out_specs=(VMEM, VMEM),
        compiler_params=near,
        cost_estimate=pl.CostEstimate(
            flops=8 * rows * pooled.shape[0] * width,
            bytes_accessed=12 * rows * width,
            transcendentals=2 * rows * pooled.shape[0] * heads,
        ),
        name="pooled",
    )(window_map, slopes, queries, pooled, other, acc_w, stat_w)
    own, stat = tie((own, stat))

    got = lax.ppermute(own, "c", SWAP)
    return pl.pallas_call(
        ref_kernel,
        out_shape=jax.ShapeDtypeStruct((rows, width), jnp.bfloat16),
        in_specs=[SMEM] + [VMEM] * 5,
        out_specs=VMEM,
        compiler_params=near,
        name="far",
    )(core.astype(jnp.int32)[None], queries, own, got, acc, stat)


def solution(mesh):
    shape = mesh.shape
    ctx = shape["ctx"]
    fine = Mesh(
        mesh.devices.reshape(shape["dp"], 2, ctx // 4, 2, shape["head"]),
        ("dp", "zh", "x", "c", "head"),
    )
    token = ("dp", "zh", "x", "c")
    return jax.shard_map(
        on_device,
        mesh=fine,
        in_specs=(
            P(token, "head"),
            P(token, "head"),
            P(token, "head"),
            P(token, None),
            P(token),
            P("dp"),
            P(token, "head", None),
            P(token, "head", None),
            P("head"),
        ),
        out_specs=P(token, "head"),
        check_vma=False,
    )
```

```python
import math

import jax
import jax.numpy as jnp
from jax import lax
from jax.experimental import pallas as pl
from jax.experimental.pallas import tpu as pltpu
from jax.sharding import Mesh, PartitionSpec as P

HD = 128
POOLS = 8
LOG2E = math.log2(math.e)
UNIT = LOG2E / math.sqrt(HD)
STRIP = 128
SWAP = [(0, 1), (1, 0)]


def dot_nt(a, b):
    return lax.dot_general(a, b, (((1,), (1,)), ((), ())), preferred_element_type=jnp.float32)


def dot_nn(a, b):
    return jnp.dot(a, b, preferred_element_type=jnp.float32)


def pool_kernel(tag_ref, seg_ref, key_ref, value_ref, out_ref):
    seg = seg_ref[...]
    member = seg == lax.broadcasted_iota(jnp.int32, (POOLS, seg.shape[1]), 0)
    count = jnp.sum(member.astype(jnp.float32), axis=1, keepdims=True)
    member = member.astype(jnp.float32).astype(jnp.bfloat16)
    width = key_ref.shape[1]
    out_ref[:, :width] = (dot_nn(member, key_ref[...]) / count).astype(jnp.bfloat16)
    out_ref[:, width : 2 * width] = (dot_nn(member, value_ref[...]) / count).astype(jnp.bfloat16)
    tag = jnp.full((POOLS, HD), tag_ref[0], jnp.int32)
    out_ref[:, 2 * width :] = tag.astype(jnp.float32).astype(jnp.bfloat16)


def soft(scores):
    top = jnp.max(scores, axis=0, keepdims=True)
    exp_terms = jnp.exp2(scores - top)
    return top, jnp.sum(exp_terms, axis=0, keepdims=True), exp_terms.astype(jnp.bfloat16)


def window_kernel(q_ref, k_ref, v_ref, acc_ref, stat_ref):
    for head in range(q_ref.shape[1] // HD):
        cols = pl.ds(head * HD, HD)
        values = v_ref[:, cols].T
        for start in range(0, q_ref.shape[0], STRIP):
            rows = pl.ds(start, STRIP)
            top, total, weights = soft(dot_nt(k_ref[:, cols], q_ref[rows, cols]) * UNIT)
            acc_ref[cols, rows] = dot_nn(values, weights)
            stat_ref[2 * head : 2 * head + 1, rows] = top
            stat_ref[2 * head + 1 : 2 * head + 2, rows] = total


def pooled_kernel(
    tag_ref, slope_ref, q_ref, pa_ref, pb_ref, acc_ref, stat_ref, acc_out_ref, stat_out_ref
):
    count, width = q_ref.shape

    def both(first):
        cols = pl.ds(first, HD)
        return jnp.concatenate([pa_ref[:, cols], pb_ref[:, cols]], axis=0)

    tags = both(2 * width).astype(jnp.float32)
    dist = jnp.abs(tags - tag_ref[0].astype(jnp.float32)) * LOG2E
    dist = jnp.concatenate([dist] * (count // HD), axis=1)
    for head in range(width // HD):
        cols = pl.ds(head * HD, HD)
        scores = dot_nt(both(head * HD), q_ref[:, cols]) * UNIT - dist * slope_ref[head]
        top, total, weights = soft(scores)
        num = dot_nn(both(width + head * HD).T, weights)
        top_n = stat_ref[2 * head : 2 * head + 1, :]
        total_n = stat_ref[2 * head + 1 : 2 * head + 2, :]
        ceiling = jnp.maximum(top_n, top)
        share_n, share = jnp.exp2(top_n - ceiling), jnp.exp2(top - ceiling)
        acc_out_ref[cols, :] = share_n * acc_ref[cols, :] + share * num
        stat_out_ref[2 * head : 2 * head + 1, :] = ceiling
        stat_out_ref[2 * head + 1 : 2 * head + 2, :] = share_n * total_n + share * total


def ref_kernel(core_ref, q_ref, own_ref, got_ref, acc_ref, stat_ref, out_ref):
    first = core_ref[0] == 0
    for head in range(q_ref.shape[1] // HD):
        cols = pl.ds(head * HD, HD)
        keys = jnp.where(first, own_ref[:, cols], got_ref[:, cols])
        values = jnp.where(first, got_ref[:, cols], own_ref[:, cols]).T
        for start in range(0, q_ref.shape[0], STRIP):
            rows = pl.ds(start, STRIP)
            top, total, weights = soft(dot_nt(keys, q_ref[rows, cols]) * UNIT)
            num = dot_nn(values, weights)
            top_n = stat_ref[2 * head : 2 * head + 1, rows]
            total_n = stat_ref[2 * head + 1 : 2 * head + 2, rows]
            ceiling = jnp.maximum(top_n, top)
            share_n, share = jnp.exp2(top_n - ceiling), jnp.exp2(top - ceiling)
            scale = 1.0 / (share_n * total_n + share * total)
            merged = (share_n * scale) * acc_ref[cols, rows] + (share * scale) * num
            out_ref[rows, cols] = merged.astype(jnp.bfloat16).T


SMEM = pl.BlockSpec(memory_space=pltpu.SMEM)
VMEM = pl.BlockSpec(memory_space=pltpu.VMEM)


def on_device(
    queries, keys, values, pool_segments, window_map, ref_owner, ref_keys, ref_values, slopes
):
    rows, width = queries.shape
    heads = width // HD
    n_zh, n_x, n_head = lax.axis_size("zh"), lax.axis_size("x"), lax.axis_size("head")
    ref_rows = ref_keys.shape[1]
    part = ref_rows // n_x
    core = lax.axis_index("c")
    owner = ref_owner[0]
    owner_c = owner % 2
    owner_x = (owner // 2) % n_x
    owner_z = owner // (2 * n_x)

    tie = lax.optimization_barrier
    near = pltpu.CompilerParams(vmem_limit_bytes=10 * 1024 * 1024)
    state = (
        jax.ShapeDtypeStruct((width, rows), jnp.float32),
        jax.ShapeDtypeStruct((16, rows), jnp.float32),
    )

    slot_k, slot_v = ref_keys[0], ref_values[0]
    given = tie(jnp.where(core == 0, slot_v, slot_k))
    got = lax.ppermute(given, "c", SWAP)
    given, slot_k, slot_v = tie((given, slot_k, slot_v))
    kept = tie(jnp.where(core == 0, slot_k, slot_v))
    mine = jnp.where(owner_c == core, kept, got)
    mine, keys_p, values_p = tie((mine, keys, values))

    spread = lax.all_to_all(mine.reshape(n_x, part, -1), "x", 0, 0, tiled=True)
    pooled = pl.pallas_call(
        pool_kernel,
        out_shape=jax.ShapeDtypeStruct((POOLS, 2 * width + HD), jnp.bfloat16),
        in_specs=[SMEM, VMEM, VMEM, VMEM],
        out_specs=VMEM,
        compiler_params=near,
        name="pool",
    )(window_map, pool_segments, keys_p, values_p)
    other = lax.ppermute(pooled, "zh", SWAP)
    piece = lax.dynamic_index_in_dim(spread, owner_x, 0, keepdims=False)
    piece = piece.reshape(part, n_head, width).transpose(1, 0, 2)
    piece = jnp.broadcast_to(piece[None], (n_zh, n_head, part, width))
    piece, pooled, other = tie((piece, pooled, other))

    turned = lax.all_to_all(
        piece.reshape(n_zh * n_head, part, width), ("zh", "head"), 0, 0, tiled=True
    )
    pooled = jnp.concatenate([pooled, other], axis=0)
    other = lax.ppermute(pooled, "x", [(i, i ^ 1) for i in range(n_x)])
    pooled = jnp.concatenate([pooled, other], axis=0)
    turned = turned.reshape(n_zh, n_head * part, width)
    block = lax.dynamic_index_in_dim(turned, owner_z, 0, keepdims=False)
    block = jnp.broadcast_to(block[None], (n_x, n_head * part, width))
    other = lax.ppermute(pooled, "x", [(i, i ^ 2) for i in range(n_x)])

    block, queries_w = tie((block, queries))

    own = lax.all_to_all(block, "x", 0, 0, tiled=True).reshape(-1, width)
    pooled = jnp.concatenate([pooled, other], axis=0)
    other = lax.ppermute(pooled, "c", SWAP)
    acc_w, stat_w = pl.pallas_call(
        window_kernel,
        out_shape=state,
        in_specs=[VMEM] * 3,
        out_specs=(VMEM, VMEM),
        compiler_params=near,
        cost_estimate=pl.CostEstimate(
            flops=4 * rows * rows * width,
            bytes_accessed=10 * rows * width,
            transcendentals=rows * rows * heads,
        ),
        name="window",
    )(queries_w, keys, values)
    acc, stat = pl.pallas_call(
        pooled_kernel,
        out_shape=state,
        in_specs=[SMEM, SMEM] + [VMEM] * 5,
        out_specs=(VMEM, VMEM),
        compiler_params=near,
        cost_estimate=pl.CostEstimate(
            flops=8 * rows * pooled.shape[0] * width,
            bytes_accessed=12 * rows * width,
            transcendentals=2 * rows * pooled.shape[0] * heads,
        ),
        name="pooled",
    )(window_map, slopes, queries, pooled, other, acc_w, stat_w)
    own, stat = tie((own, stat))

    got = lax.ppermute(own, "c", SWAP)
    return pl.pallas_call(
        ref_kernel,
        out_shape=jax.ShapeDtypeStruct((rows, width), jnp.bfloat16),
        in_specs=[SMEM] + [VMEM] * 5,
        out_specs=VMEM,
        compiler_params=near,
        name="far",
    )(core.astype(jnp.int32)[None], queries, own, got, acc, stat)


def solution(mesh):
    shape = mesh.shape
    ctx = shape["ctx"]
    fine = Mesh(
        mesh.devices.reshape(shape["dp"], 2, ctx // 4, 2, shape["head"]),
        ("dp", "zh", "x", "c", "head"),
    )
    token = ("dp", "zh", "x", "c")
    return jax.shard_map(
        on_device,
        mesh=fine,
        in_specs=(
            P(token, "head"),
            P(token, "head"),
            P(token, "head"),
            P(token, None),
            P(token),
            P("dp"),
            P(token, "head", None),
            P(token, "head", None),
            P("head"),
        ),
        out_specs=P(token, "head"),
        check_vma=False,
    )
```

```python
import functools
import math

import jax
import jax.numpy as jnp
from jax import lax
from jax.experimental import pallas as pl
from jax.experimental.pallas import tpu as pltpu
from jax.sharding import Mesh, PartitionSpec as P

HD = 128
POOLS = 8
LOG2E = math.log2(math.e)
UNIT = LOG2E / math.sqrt(HD)
STRIP = 128
SWAP = [(0, 1), (1, 0)]


def dot_nt(a, b):
    return lax.dot_general(a, b, (((1,), (1,)), ((), ())), preferred_element_type=jnp.float32)


def dot_nn(a, b):
    return jnp.dot(a, b, preferred_element_type=jnp.float32)


def pool_kernel(tag_ref, seg_ref, key_ref, value_ref, out_ref):
    seg = seg_ref[...]
    member = seg == lax.broadcasted_iota(jnp.int32, (POOLS, seg.shape[1]), 0)
    count = jnp.sum(member.astype(jnp.float32), axis=1, keepdims=True)
    member = member.astype(jnp.float32).astype(jnp.bfloat16)
    width = key_ref.shape[1]
    out_ref[:, :width] = (dot_nn(member, key_ref[...]) / count).astype(jnp.bfloat16)
    out_ref[:, width : 2 * width] = (dot_nn(member, value_ref[...]) / count).astype(jnp.bfloat16)
    tag = jnp.full((POOLS, HD), tag_ref[0], jnp.int32)
    out_ref[:, 2 * width :] = tag.astype(jnp.float32).astype(jnp.bfloat16)


def soft(scores):
    top = jnp.max(scores, axis=0, keepdims=True)
    exp_terms = jnp.exp2(scores - top)
    return top, jnp.sum(exp_terms, axis=0, keepdims=True), exp_terms.astype(jnp.bfloat16)


def window_kernel(q_ref, k_ref, v_ref, acc_ref, stat_ref):
    for head in range(q_ref.shape[1] // HD):
        cols = pl.ds(head * HD, HD)
        values = v_ref[:, cols].T
        for start in range(0, q_ref.shape[0], STRIP):
            rows = pl.ds(start, STRIP)
            top, total, weights = soft(dot_nt(k_ref[:, cols], q_ref[rows, cols]) * UNIT)
            acc_ref[cols, rows] = dot_nn(values, weights)
            stat_ref[2 * head : 2 * head + 1, rows] = top
            stat_ref[2 * head + 1 : 2 * head + 2, rows] = total


def pooled_kernel(
    tag_ref, slope_ref, q_ref, pa_ref, pb_ref, acc_ref, stat_ref, acc_out_ref, stat_out_ref
):
    count, width = q_ref.shape

    def both(first):
        cols = pl.ds(first, HD)
        return jnp.concatenate([pa_ref[:, cols], pb_ref[:, cols]], axis=0)

    tags = both(2 * width).astype(jnp.float32)
    dist = jnp.abs(tags - tag_ref[0].astype(jnp.float32)) * LOG2E
    dist = jnp.concatenate([dist] * (count // HD), axis=1)
    for head in range(width // HD):
        cols = pl.ds(head * HD, HD)
        scores = dot_nt(both(head * HD), q_ref[:, cols]) * UNIT - dist * slope_ref[head]
        top, total, weights = soft(scores)
        num = dot_nn(both(width + head * HD).T, weights)
        top_n = stat_ref[2 * head : 2 * head + 1, :]
        total_n = stat_ref[2 * head + 1 : 2 * head + 2, :]
        ceiling = jnp.maximum(top_n, top)
        share_n, share = jnp.exp2(top_n - ceiling), jnp.exp2(top - ceiling)
        acc_out_ref[cols, :] = share_n * acc_ref[cols, :] + share * num
        stat_out_ref[2 * head : 2 * head + 1, :] = ceiling
        stat_out_ref[2 * head + 1 : 2 * head + 2, :] = share_n * total_n + share * total


def split_kernel(side_ref, k_ref, v_ref, out_ref):
    groups, half = out_ref.shape[1], out_ref.shape[4]

    def move(side):
        for kind, src in enumerate((k_ref, v_ref)):
            for group in range(groups):
                out_ref[:, group, kind] = src[:, :, pl.ds((2 * group + side) * half, half)]

    for side in range(2):
        pl.when(side_ref[0] == side)(functools.partial(move, side))


def ref_heads(q_ref, kv_ref, acc_ref, stat_ref, side, write):
    count = kv_ref.shape[3] // HD
    for local in range(count):
        head = side * count + local
        cols, lanes = pl.ds(head * HD, HD), pl.ds(local * HD, HD)
        keys = kv_ref[:, 0, :, lanes].reshape(-1, HD)
        values = kv_ref[:, 1, :, lanes].reshape(-1, HD).T
        for start in range(0, q_ref.shape[0], STRIP):
            rows = pl.ds(start, STRIP)
            top, total, weights = soft(dot_nt(keys, q_ref[rows, cols]) * UNIT)
            num = dot_nn(values, weights)
            top_n = stat_ref[2 * head : 2 * head + 1, rows]
            total_n = stat_ref[2 * head + 1 : 2 * head + 2, rows]
            ceiling = jnp.maximum(top_n, top)
            share_n, share = jnp.exp2(top_n - ceiling), jnp.exp2(top - ceiling)
            scale = 1.0 / (share_n * total_n + share * total)
            merged = (share_n * scale) * acc_ref[cols, rows] + (share * scale) * num
            write(rows, cols, lanes, merged.astype(jnp.bfloat16).T)


def own_kernel(core_ref, q_ref, kv_ref, acc_ref, stat_ref, part_ref):
    def write(rows, cols, lanes, block):
        part_ref[rows, lanes] = block

    for side in range(2):
        pl.when(core_ref[0] == side)(
            functools.partial(ref_heads, q_ref, kv_ref, acc_ref, stat_ref, side, write)
        )


def got_kernel(core_ref, q_ref, kv_ref, acc_ref, stat_ref, part_ref, out_ref):
    half = part_ref.shape[1]

    def write(rows, cols, lanes, block):
        out_ref[rows, cols] = block

    def finish(side):
        out_ref[:, side * half : (side + 1) * half] = part_ref[...]
        ref_heads(q_ref, kv_ref, acc_ref, stat_ref, 1 - side, write)

    for side in range(2):
        pl.when(core_ref[0] == side)(functools.partial(finish, side))


SMEM = pl.BlockSpec(memory_space=pltpu.SMEM)
VMEM = pl.BlockSpec(memory_space=pltpu.VMEM)


def on_device(
    queries, keys, values, pool_segments, window_map, ref_owner, ref_keys, ref_values, slopes
):
    rows, width = queries.shape
    heads = width // HD
    n_zh, n_x, n_head = lax.axis_size("zh"), lax.axis_size("x"), lax.axis_size("head")
    ref_rows = ref_keys.shape[1]
    part = ref_rows // n_x
    core = lax.axis_index("c")
    owner = ref_owner[0]
    owner_c = owner % 2
    owner_x = (owner // 2) % n_x
    owner_z = owner // (2 * n_x)

    tie = lax.optimization_barrier
    near = pltpu.CompilerParams(vmem_limit_bytes=10 * 1024 * 1024)
    state = (
        jax.ShapeDtypeStruct((width, rows), jnp.float32),
        jax.ShapeDtypeStruct((16, rows), jnp.float32),
    )

    slot_k = ref_keys[0].reshape(n_x, part, -1)
    slot_v = ref_values[0].reshape(n_x, part, -1)
    half = width // 2
    side = core.astype(jnp.int32)[None]
    split = pl.pallas_call(
        split_kernel,
        out_shape=jax.ShapeDtypeStruct((n_x, n_head, 2, part, half), jnp.bfloat16),
        in_specs=[SMEM, VMEM, VMEM],
        out_specs=VMEM,
        compiler_params=near,
        name="split",
    )
    given = split(1 - side, slot_k, slot_v)
    got = lax.ppermute(given, "c", SWAP)
    given, slot_k, slot_v = tie((given, slot_k, slot_v))
    kept = tie(split(side, slot_k, slot_v))
    mine = jnp.where(owner_c == core, kept, got)
    mine, keys_p, values_p = tie((mine, keys, values))

    spread = lax.all_to_all(mine.reshape(n_x, -1, half), "x", 0, 0, tiled=True)
    pooled = pl.pallas_call(
        pool_kernel,
        out_shape=jax.ShapeDtypeStruct((POOLS, 2 * width + HD), jnp.bfloat16),
        in_specs=[SMEM, VMEM, VMEM, VMEM],
        out_specs=VMEM,
        compiler_params=near,
        name="pool",
    )(window_map, pool_segments, keys_p, values_p)
    other = lax.ppermute(pooled, "zh", SWAP)
    piece = lax.dynamic_index_in_dim(spread, owner_x, 0, keepdims=False)
    piece = piece.reshape(n_head, 2 * part, half)
    piece = jnp.broadcast_to(piece[None], (n_zh, n_head, 2 * part, half))
    piece, pooled, other = tie((piece, pooled, other))

    turned = lax.all_to_all(
        piece.reshape(n_zh * n_head, 2 * part, half), ("zh", "head"), 0, 0, tiled=True
    )
    pooled = jnp.concatenate([pooled, other], axis=0)
    other = lax.ppermute(pooled, "x", [(i, i ^ 1) for i in range(n_x)])
    pooled = jnp.concatenate([pooled, other], axis=0)
    turned = turned.reshape(n_zh, n_head * 2 * part, half)
    block = lax.dynamic_index_in_dim(turned, owner_z, 0, keepdims=False)
    block = jnp.broadcast_to(block[None], (n_x, n_head * 2 * part, half))
    other = lax.ppermute(pooled, "x", [(i, i ^ 2) for i in range(n_x)])

    block, queries_w = tie((block, queries))

    own = lax.all_to_all(block, "x", 0, 0, tiled=True).reshape(-1, 2, part, half)
    pooled = jnp.concatenate([pooled, other], axis=0)
    other = lax.ppermute(pooled, "c", SWAP)
    acc_w, stat_w = pl.pallas_call(
        window_kernel,
        out_shape=state,
        in_specs=[VMEM] * 3,
        out_specs=(VMEM, VMEM),
        compiler_params=near,
        cost_estimate=pl.CostEstimate(
            flops=4 * rows * rows * width,
            bytes_accessed=10 * rows * width,
            transcendentals=rows * rows * heads,
        ),
        name="window",
    )(queries_w, keys, values)
    acc, stat = pl.pallas_call(
        pooled_kernel,
        out_shape=state,
        in_specs=[SMEM, SMEM] + [VMEM] * 5,
        out_specs=(VMEM, VMEM),
        compiler_params=near,
        cost_estimate=pl.CostEstimate(
            flops=8 * rows * pooled.shape[0] * width,
            bytes_accessed=12 * rows * width,
            transcendentals=2 * rows * pooled.shape[0] * heads,
        ),
        name="pooled",
    )(window_map, slopes, queries, pooled, other, acc_w, stat_w)
    own, stat = tie((own, stat))

    got = lax.ppermute(own, "c", SWAP)
    out = pl.pallas_call(
        own_kernel,
        out_shape=jax.ShapeDtypeStruct((rows, half), jnp.bfloat16),
        in_specs=[SMEM] + [VMEM] * 4,
        out_specs=VMEM,
        compiler_params=near,
        cost_estimate=pl.CostEstimate(
            flops=2 * rows * rows * width,
            bytes_accessed=5 * rows * width,
            transcendentals=rows * rows * heads // 2,
        ),
        name="own",
    )(side, queries, own, acc, stat)
    return pl.pallas_call(
        got_kernel,
        out_shape=jax.ShapeDtypeStruct((rows, width), jnp.bfloat16),
        in_specs=[SMEM] + [VMEM] * 5,
        out_specs=VMEM,
        compiler_params=near,
        name="got",
    )(side, queries, got, acc, stat, out)


def solution(mesh):
    shape = mesh.shape
    ctx = shape["ctx"]
    fine = Mesh(
        mesh.devices.reshape(shape["dp"], 2, ctx // 4, 2, shape["head"]),
        ("dp", "zh", "x", "c", "head"),
    )
    token = ("dp", "zh", "x", "c")
    return jax.shard_map(
        on_device,
        mesh=fine,
        in_specs=(
            P(token, "head"),
            P(token, "head"),
            P(token, "head"),
            P(token, None),
            P(token),
            P("dp"),
            P(token, "head", None),
            P(token, "head", None),
            P("head"),
        ),
        out_specs=P(token, "head"),
        check_vma=False,
    )
```

```python
import functools
import math

import jax
import jax.numpy as jnp
from jax import lax
from jax.experimental import pallas as pl
from jax.experimental.pallas import tpu as pltpu
from jax.sharding import Mesh, PartitionSpec as P

HD = 128
POOLS = 8
LOG2E = math.log2(math.e)
UNIT = LOG2E / math.sqrt(HD)
STRIP = 128
SWAP = [(0, 1), (1, 0)]


def dot_nt(a, b):
    return lax.dot_general(a, b, (((1,), (1,)), ((), ())), preferred_element_type=jnp.float32)


def dot_nn(a, b):
    return jnp.dot(a, b, preferred_element_type=jnp.float32)


def pool_kernel(tag_ref, seg_ref, key_ref, value_ref, out_ref):
    seg = seg_ref[...]
    member = seg == lax.broadcasted_iota(jnp.int32, (POOLS, seg.shape[1]), 0)
    count = jnp.sum(member.astype(jnp.float32), axis=1, keepdims=True)
    member = member.astype(jnp.float32).astype(jnp.bfloat16)
    width = key_ref.shape[1]
    out_ref[:, :width] = (dot_nn(member, key_ref[...]) / count).astype(jnp.bfloat16)
    out_ref[:, width : 2 * width] = (dot_nn(member, value_ref[...]) / count).astype(jnp.bfloat16)
    tag = jnp.full((POOLS, HD), tag_ref[0], jnp.int32)
    out_ref[:, 2 * width :] = tag.astype(jnp.float32).astype(jnp.bfloat16)


def soft(scores):
    top = jnp.max(scores, axis=0, keepdims=True)
    exp_terms = jnp.exp2(scores - top)
    return top, jnp.sum(exp_terms, axis=0, keepdims=True), exp_terms.astype(jnp.bfloat16)


def window_kernel(q_ref, k_ref, v_ref, acc_ref, stat_ref):
    for head in range(q_ref.shape[1] // HD):
        cols = pl.ds(head * HD, HD)
        values = v_ref[:, cols].T
        for start in range(0, q_ref.shape[0], STRIP):
            rows = pl.ds(start, STRIP)
            top, total, weights = soft(dot_nt(k_ref[:, cols], q_ref[rows, cols]) * UNIT)
            acc_ref[cols, rows] = dot_nn(values, weights)
            stat_ref[2 * head : 2 * head + 1, rows] = top
            stat_ref[2 * head + 1 : 2 * head + 2, rows] = total


def pooled_kernel(
    tag_ref, slope_ref, q_ref, pa_ref, pb_ref, acc_ref, stat_ref, acc_out_ref, stat_out_ref
):
    count, width = q_ref.shape

    def both(first):
        cols = pl.ds(first, HD)
        return jnp.concatenate([pa_ref[:, cols], pb_ref[:, cols]], axis=0)

    tags = both(2 * width).astype(jnp.float32)
    dist = jnp.abs(tags - tag_ref[0].astype(jnp.float32)) * LOG2E
    dist = jnp.concatenate([dist] * (count // HD), axis=1)
    for head in range(width // HD):
        cols = pl.ds(head * HD, HD)
        scores = dot_nt(both(head * HD), q_ref[:, cols]) * UNIT - dist * slope_ref[head]
        top, total, weights = soft(scores)
        num = dot_nn(both(width + head * HD).T, weights)
        top_n = stat_ref[2 * head : 2 * head + 1, :]
        total_n = stat_ref[2 * head + 1 : 2 * head + 2, :]
        ceiling = jnp.maximum(top_n, top)
        share_n, share = jnp.exp2(top_n - ceiling), jnp.exp2(top - ceiling)
        acc_out_ref[cols, :] = share_n * acc_ref[cols, :] + share * num
        stat_out_ref[2 * head : 2 * head + 1, :] = ceiling
        stat_out_ref[2 * head + 1 : 2 * head + 2, :] = share_n * total_n + share * total


def split_kernel(side_ref, k_ref, v_ref, out_ref):
    groups, half = out_ref.shape[1], out_ref.shape[4]

    def move(side):
        for kind, src in enumerate((k_ref, v_ref)):
            for group in range(groups):
                out_ref[:, group, kind] = src[:, :, pl.ds((2 * group + side) * half, half)]

    for side in range(2):
        pl.when(side_ref[0] == side)(functools.partial(move, side))


def give_kernel(side_ref, k_ref, v_ref, out_ref, buf, in_sems, out_sems):
    groups, half = out_ref.shape[1], out_ref.shape[4]

    def move(side):
        pairs = [
            (
                pltpu.make_async_copy(
                    src.at[:, :, pl.ds((2 * group + side) * half, half)],
                    buf.at[:, group, kind],
                    in_sems.at[kind, group],
                ),
                pltpu.make_async_copy(
                    buf.at[:, group, kind], out_ref.at[:, group, kind], out_sems.at[kind, group]
                ),
            )
            for kind, src in enumerate((k_ref, v_ref))
            for group in range(groups)
        ]
        for fetch, _ in pairs:
            fetch.start()
        for fetch, store in pairs:
            fetch.wait()
            store.start()
        for _, store in pairs:
            store.wait()

    for side in range(2):
        pl.when(side_ref[0] == side)(functools.partial(move, side))


def ref_heads(q_ref, kv_ref, acc_ref, stat_ref, side, write):
    count = kv_ref.shape[3] // HD
    for local in range(count):
        head = side * count + local
        cols, lanes = pl.ds(head * HD, HD), pl.ds(local * HD, HD)
        keys = kv_ref[:, 0, :, lanes].reshape(-1, HD)
        values = kv_ref[:, 1, :, lanes].reshape(-1, HD).T
        for start in range(0, q_ref.shape[0], STRIP):
            rows = pl.ds(start, STRIP)
            top, total, weights = soft(dot_nt(keys, q_ref[rows, cols]) * UNIT)
            num = dot_nn(values, weights)
            top_n = stat_ref[2 * head : 2 * head + 1, rows]
            total_n = stat_ref[2 * head + 1 : 2 * head + 2, rows]
            ceiling = jnp.maximum(top_n, top)
            share_n, share = jnp.exp2(top_n - ceiling), jnp.exp2(top - ceiling)
            scale = 1.0 / (share_n * total_n + share * total)
            merged = (share_n * scale) * acc_ref[cols, rows] + (share * scale) * num
            write(rows, cols, lanes, merged.astype(jnp.bfloat16).T)


def own_kernel(core_ref, q_ref, kv_ref, acc_ref, stat_ref, part_ref):
    def write(rows, cols, lanes, block):
        part_ref[rows, lanes] = block

    for side in range(2):
        pl.when(core_ref[0] == side)(
            functools.partial(ref_heads, q_ref, kv_ref, acc_ref, stat_ref, side, write)
        )


def got_kernel(core_ref, q_ref, kv_ref, acc_ref, stat_ref, part_ref, out_ref, buf, sems):
    half = part_ref.shape[1]

    def finish(side):
        done = [
            pltpu.make_async_copy(
                part_ref, out_ref.at[:, pl.ds(side * half, half)], sems.at[half // HD]
            )
        ]
        done[0].start()

        def write(rows, cols, lanes, block):
            buf[rows, lanes] = block
            if rows.start + rows.size == buf.shape[0]:
                copy = pltpu.make_async_copy(
                    buf.at[:, lanes], out_ref.at[:, cols], sems.at[lanes.start // HD]
                )
                copy.start()
                done.append(copy)

        ref_heads(q_ref, kv_ref, acc_ref, stat_ref, 1 - side, write)
        for copy in done:
            copy.wait()

    for side in range(2):
        pl.when(core_ref[0] == side)(functools.partial(finish, side))


SMEM = pl.BlockSpec(memory_space=pltpu.SMEM)
VMEM = pl.BlockSpec(memory_space=pltpu.VMEM)
ANY = pl.BlockSpec(memory_space=pl.ANY)
GRANT = 63600 * 1024


def on_device(
    queries, keys, values, pool_segments, window_map, ref_owner, ref_keys, ref_values, slopes
):
    rows, width = queries.shape
    heads = width // HD
    n_zh, n_x, n_head = lax.axis_size("zh"), lax.axis_size("x"), lax.axis_size("head")
    ref_rows = ref_keys.shape[1]
    part = ref_rows // n_x
    core = lax.axis_index("c")
    owner = ref_owner[0]
    owner_c = owner % 2
    owner_x = (owner // 2) % n_x
    owner_z = owner // (2 * n_x)

    tie = lax.optimization_barrier
    near = pltpu.CompilerParams(vmem_limit_bytes=10 * 1024 * 1024)
    state = (
        jax.ShapeDtypeStruct((width, rows), jnp.float32),
        jax.ShapeDtypeStruct((16, rows), jnp.float32),
    )

    slot_k = ref_keys[0].reshape(n_x, part, -1)
    slot_v = ref_values[0].reshape(n_x, part, -1)
    half = width // 2
    side = core.astype(jnp.int32)[None]
    split = pl.pallas_call(
        split_kernel,
        out_shape=jax.ShapeDtypeStruct((n_x, n_head, 2, part, half), jnp.bfloat16),
        in_specs=[SMEM, VMEM, VMEM],
        out_specs=VMEM,
        compiler_params=near,
        name="split",
    )
    given = pl.pallas_call(
        give_kernel,
        out_shape=jax.ShapeDtypeStruct((n_x, n_head, 2, part, half), jnp.bfloat16),
        in_specs=[SMEM, ANY, ANY],
        out_specs=ANY,
        scratch_shapes=[
            pltpu.VMEM((n_x, n_head, 2, part, half), jnp.bfloat16),
            pltpu.SemaphoreType.DMA((2, n_head)),
            pltpu.SemaphoreType.DMA((2, n_head)),
        ],
        compiler_params=pltpu.CompilerParams(vmem_limit_bytes=GRANT),
        name="give",
    )(1 - side, slot_k, slot_v)
    got = lax.ppermute(given, "c", SWAP)
    given, slot_k, slot_v = tie((given, slot_k, slot_v))
    kept = tie(split(side, slot_k, slot_v))
    mine = jnp.where(owner_c == core, kept, got)
    mine, keys_p, values_p = tie((mine, keys, values))

    spread = lax.all_to_all(mine.reshape(n_x, -1, half), "x", 0, 0, tiled=True)
    pooled = pl.pallas_call(
        pool_kernel,
        out_shape=jax.ShapeDtypeStruct((POOLS, 2 * width + HD), jnp.bfloat16),
        in_specs=[SMEM, VMEM, VMEM, VMEM],
        out_specs=VMEM,
        compiler_params=near,
        name="pool",
    )(window_map, pool_segments, keys_p, values_p)
    other = lax.ppermute(pooled, "zh", SWAP)
    piece = lax.dynamic_index_in_dim(spread, owner_x, 0, keepdims=False)
    piece = piece.reshape(n_head, 2 * part, half)
    piece = jnp.broadcast_to(piece[None], (n_zh, n_head, 2 * part, half))
    piece, pooled, other = tie((piece, pooled, other))

    turned = lax.all_to_all(
        piece.reshape(n_zh * n_head, 2 * part, half), ("zh", "head"), 0, 0, tiled=True
    )
    pooled = jnp.concatenate([pooled, other], axis=0)
    other = lax.ppermute(pooled, "x", [(i, i ^ 1) for i in range(n_x)])
    pooled = jnp.concatenate([pooled, other], axis=0)
    turned = turned.reshape(n_zh, n_head * 2 * part, half)
    block = lax.dynamic_index_in_dim(turned, owner_z, 0, keepdims=False)
    block = jnp.broadcast_to(block[None], (n_x, n_head * 2 * part, half))
    other = lax.ppermute(pooled, "x", [(i, i ^ 2) for i in range(n_x)])

    block, queries_w = tie((block, queries))

    own = lax.all_to_all(block, "x", 0, 0, tiled=True).reshape(-1, 2, part, half)
    pooled = jnp.concatenate([pooled, other], axis=0)
    other = lax.ppermute(pooled, "c", SWAP)
    acc_w, stat_w = pl.pallas_call(
        window_kernel,
        out_shape=state,
        in_specs=[VMEM] * 3,
        out_specs=(VMEM, VMEM),
        compiler_params=near,
        cost_estimate=pl.CostEstimate(
            flops=4 * rows * rows * width,
            bytes_accessed=10 * rows * width,
            transcendentals=rows * rows * heads,
        ),
        name="window",
    )(queries_w, keys, values)
    acc, stat = pl.pallas_call(
        pooled_kernel,
        out_shape=state,
        in_specs=[SMEM, SMEM] + [VMEM] * 5,
        out_specs=(VMEM, VMEM),
        compiler_params=near,
        cost_estimate=pl.CostEstimate(
            flops=8 * rows * pooled.shape[0] * width,
            bytes_accessed=12 * rows * width,
            transcendentals=2 * rows * pooled.shape[0] * heads,
        ),
        name="pooled",
    )(window_map, slopes, queries, pooled, other, acc_w, stat_w)
    own, stat = tie((own, stat))

    got = lax.ppermute(own, "c", SWAP)
    out = pl.pallas_call(
        own_kernel,
        out_shape=jax.ShapeDtypeStruct((rows, half), jnp.bfloat16),
        in_specs=[SMEM] + [VMEM] * 4,
        out_specs=VMEM,
        compiler_params=near,
        cost_estimate=pl.CostEstimate(
            flops=2 * rows * rows * width,
            bytes_accessed=5 * rows * width,
            transcendentals=rows * rows * heads // 2,
        ),
        name="own",
    )(side, queries, own, acc, stat)
    return pl.pallas_call(
        got_kernel,
        out_shape=jax.ShapeDtypeStruct((rows, width), jnp.bfloat16),
        in_specs=[SMEM] + [VMEM] * 5,
        out_specs=ANY,
        scratch_shapes=[
            pltpu.VMEM((rows, half), jnp.bfloat16),
            pltpu.SemaphoreType.DMA((half // HD + 1,)),
        ],
        compiler_params=near,
        name="got",
    )(side, queries, got, acc, stat, out)


def solution(mesh):
    shape = mesh.shape
    ctx = shape["ctx"]
    fine = Mesh(
        mesh.devices.reshape(shape["dp"], 2, ctx // 4, 2, shape["head"]),
        ("dp", "zh", "x", "c", "head"),
    )
    token = ("dp", "zh", "x", "c")
    return jax.shard_map(
        on_device,
        mesh=fine,
        in_specs=(
            P(token, "head"),
            P(token, "head"),
            P(token, "head"),
            P(token, None),
            P(token),
            P("dp"),
            P(token, "head", None),
            P(token, "head", None),
            P("head"),
        ),
        out_specs=P(token, "head"),
        check_vma=False,
    )
```

```python
import functools
import math

import jax
import jax.numpy as jnp
from jax import lax
from jax.experimental import pallas as pl
from jax.experimental.pallas import tpu as pltpu
from jax.sharding import Mesh, PartitionSpec as P

HD = 128
POOLS = 8
LOG2E = math.log2(math.e)
UNIT = LOG2E / math.sqrt(HD)
STRIP = 128
SWAP = [(0, 1), (1, 0)]


def dot_nt(a, b):
    return lax.dot_general(a, b, (((1,), (1,)), ((), ())), preferred_element_type=jnp.float32)


def dot_nn(a, b):
    return jnp.dot(a, b, preferred_element_type=jnp.float32)


def pool_kernel(tag_ref, seg_ref, key_ref, value_ref, out_ref):
    seg = seg_ref[...]
    member = seg == lax.broadcasted_iota(jnp.int32, (POOLS, seg.shape[1]), 0)
    count = jnp.sum(member.astype(jnp.float32), axis=1, keepdims=True)
    member = member.astype(jnp.float32).astype(jnp.bfloat16)
    width = key_ref.shape[1]
    out_ref[:, :width] = (dot_nn(member, key_ref[...]) / count).astype(jnp.bfloat16)
    out_ref[:, width : 2 * width] = (dot_nn(member, value_ref[...]) / count).astype(jnp.bfloat16)
    tag = jnp.full((POOLS, HD), tag_ref[0], jnp.int32)
    out_ref[:, 2 * width :] = tag.astype(jnp.float32).astype(jnp.bfloat16)


def soft(scores):
    top = jnp.max(scores, axis=0, keepdims=True)
    exp_terms = jnp.exp2(scores - top)
    return top, jnp.sum(exp_terms, axis=0, keepdims=True), exp_terms.astype(jnp.bfloat16)


def window_kernel(q_ref, k_ref, v_ref, acc_ref, stat_ref):
    for head in range(q_ref.shape[1] // HD):
        cols = pl.ds(head * HD, HD)
        values = v_ref[:, cols].T
        for start in range(0, q_ref.shape[0], STRIP):
            rows = pl.ds(start, STRIP)
            top, total, weights = soft(dot_nt(k_ref[:, cols], q_ref[rows, cols]) * UNIT)
            acc_ref[cols, rows] = dot_nn(values, weights)
            stat_ref[2 * head : 2 * head + 1, rows] = top
            stat_ref[2 * head + 1 : 2 * head + 2, rows] = total


def pooled_kernel(
    tag_ref, slope_ref, q_ref, pa_ref, pb_ref, acc_ref, stat_ref, acc_out_ref, stat_out_ref
):
    count, width = q_ref.shape

    def both(first):
        cols = pl.ds(first, HD)
        return jnp.concatenate([pa_ref[:, cols], pb_ref[:, cols]], axis=0)

    tags = both(2 * width).astype(jnp.float32)
    dist = jnp.abs(tags - tag_ref[0].astype(jnp.float32)) * LOG2E
    dist = jnp.concatenate([dist] * (count // HD), axis=1)
    for head in range(width // HD):
        cols = pl.ds(head * HD, HD)
        scores = dot_nt(both(head * HD), q_ref[:, cols]) * UNIT - dist * slope_ref[head]
        top, total, weights = soft(scores)
        num = dot_nn(both(width + head * HD).T, weights)
        top_n = stat_ref[2 * head : 2 * head + 1, :]
        total_n = stat_ref[2 * head + 1 : 2 * head + 2, :]
        ceiling = jnp.maximum(top_n, top)
        share_n, share = jnp.exp2(top_n - ceiling), jnp.exp2(top - ceiling)
        acc_out_ref[cols, :] = share_n * acc_ref[cols, :] + share * num
        stat_out_ref[2 * head : 2 * head + 1, :] = ceiling
        stat_out_ref[2 * head + 1 : 2 * head + 2, :] = share_n * total_n + share * total


def split_kernel(side_ref, k_ref, v_ref, out_ref):
    groups, half = out_ref.shape[1], out_ref.shape[4]

    def move(side):
        for kind, src in enumerate((k_ref, v_ref)):
            for group in range(groups):
                out_ref[:, group, kind] = src[:, :, pl.ds((2 * group + side) * half, half)]

    for side in range(2):
        pl.when(side_ref[0] == side)(functools.partial(move, side))


def give_kernel(side_ref, k_ref, v_ref, out_ref, buf, in_sems, out_sems):
    groups, half = out_ref.shape[1], out_ref.shape[4]

    def move(side):
        pairs = [
            (
                pltpu.make_async_copy(
                    src.at[:, :, pl.ds((2 * group + side) * half, half)],
                    buf.at[:, group, kind],
                    in_sems.at[kind, group],
                ),
                pltpu.make_async_copy(
                    buf.at[:, group, kind], out_ref.at[:, group, kind], out_sems.at[kind, group]
                ),
            )
            for kind, src in enumerate((k_ref, v_ref))
            for group in range(groups)
        ]
        for fetch, _ in pairs:
            fetch.start()
        for fetch, store in pairs:
            fetch.wait()
            store.start()
        for _, store in pairs:
            store.wait()

    for side in range(2):
        pl.when(side_ref[0] == side)(functools.partial(move, side))


def ref_heads(q_ref, kv_ref, acc_ref, stat_ref, side, write):
    count = kv_ref.shape[3] // HD
    for local in range(count):
        head = side * count + local
        cols, lanes = pl.ds(head * HD, HD), pl.ds(local * HD, HD)
        keys = kv_ref[:, 0, :, lanes].reshape(-1, HD)
        values = kv_ref[:, 1, :, lanes].reshape(-1, HD).T
        for start in range(0, q_ref.shape[0], STRIP):
            rows = pl.ds(start, STRIP)
            top, total, weights = soft(dot_nt(keys, q_ref[rows, cols]) * UNIT)
            num = dot_nn(values, weights)
            top_n = stat_ref[2 * head : 2 * head + 1, rows]
            total_n = stat_ref[2 * head + 1 : 2 * head + 2, rows]
            ceiling = jnp.maximum(top_n, top)
            share_n, share = jnp.exp2(top_n - ceiling), jnp.exp2(top - ceiling)
            scale = 1.0 / (share_n * total_n + share * total)
            merged = (share_n * scale) * acc_ref[cols, rows] + (share * scale) * num
            write(rows, cols, lanes, merged.astype(jnp.bfloat16).T)


def own_kernel(core_ref, q_ref, kv_ref, acc_ref, stat_ref, part_ref):
    def write(rows, cols, lanes, block):
        part_ref[rows, lanes] = block

    for side in range(2):
        pl.when(core_ref[0] == side)(
            functools.partial(ref_heads, q_ref, kv_ref, acc_ref, stat_ref, side, write)
        )


def got_kernel(core_ref, q_ref, kv_ref, acc_ref, stat_ref, part_ref, out_ref, buf, sems):
    half = part_ref.shape[1]

    def finish(side):
        done = [
            pltpu.make_async_copy(
                part_ref, out_ref.at[:, pl.ds(side * half, half)], sems.at[half // HD]
            )
        ]
        done[0].start()

        def write(rows, cols, lanes, block):
            buf[rows, lanes] = block
            if rows.start + rows.size == buf.shape[0]:
                copy = pltpu.make_async_copy(
                    buf.at[:, lanes], out_ref.at[:, cols], sems.at[lanes.start // HD]
                )
                copy.start()
                done.append(copy)

        ref_heads(q_ref, kv_ref, acc_ref, stat_ref, 1 - side, write)
        for copy in done:
            copy.wait()

    for side in range(2):
        pl.when(core_ref[0] == side)(functools.partial(finish, side))


SMEM = pl.BlockSpec(memory_space=pltpu.SMEM)
VMEM = pl.BlockSpec(memory_space=pltpu.VMEM)
ANY = pl.BlockSpec(memory_space=pl.ANY)
GRANT = 64900 * 1024


def on_device(
    queries, keys, values, pool_segments, window_map, ref_owner, ref_keys, ref_values, slopes
):
    rows, width = queries.shape
    heads = width // HD
    n_zh, n_x, n_head = lax.axis_size("zh"), lax.axis_size("x"), lax.axis_size("head")
    ref_rows = ref_keys.shape[1]
    part = ref_rows // n_x
    core = lax.axis_index("c")
    owner = ref_owner[0]
    owner_c = owner % 2
    owner_x = (owner // 2) % n_x
    owner_z = owner // (2 * n_x)

    tie = lax.optimization_barrier
    near = pltpu.CompilerParams(vmem_limit_bytes=10 * 1024 * 1024)
    state = (
        jax.ShapeDtypeStruct((width, rows), jnp.float32),
        jax.ShapeDtypeStruct((16, rows), jnp.float32),
    )

    slot_k = ref_keys[0].reshape(n_x, part, -1)
    slot_v = ref_values[0].reshape(n_x, part, -1)
    half = width // 2
    side = core.astype(jnp.int32)[None]
    split = pl.pallas_call(
        split_kernel,
        out_shape=jax.ShapeDtypeStruct((n_x, n_head, 2, part, half), jnp.bfloat16),
        in_specs=[SMEM, VMEM, VMEM],
        out_specs=VMEM,
        compiler_params=near,
        name="split",
    )
    given = pl.pallas_call(
        give_kernel,
        out_shape=jax.ShapeDtypeStruct((n_x, n_head, 2, part, half), jnp.bfloat16),
        in_specs=[SMEM, ANY, ANY],
        out_specs=ANY,
        scratch_shapes=[
            pltpu.VMEM((n_x, n_head, 2, part, half), jnp.bfloat16),
            pltpu.SemaphoreType.DMA((2, n_head)),
            pltpu.SemaphoreType.DMA((2, n_head)),
        ],
        compiler_params=pltpu.CompilerParams(vmem_limit_bytes=GRANT),
        name="give",
    )(1 - side, slot_k, slot_v)
    got = lax.ppermute(given, "c", SWAP)
    given, slot_k, slot_v = tie((given, slot_k, slot_v))
    kept = tie(split(side, slot_k, slot_v))
    mine = jnp.where(owner_c == core, kept, got)
    mine, keys_p, values_p = tie((mine, keys, values))

    spread = lax.all_to_all(mine.reshape(n_x, -1, half), "x", 0, 0, tiled=True)
    pooled = pl.pallas_call(
        pool_kernel,
        out_shape=jax.ShapeDtypeStruct((POOLS, 2 * width + HD), jnp.bfloat16),
        in_specs=[SMEM, VMEM, VMEM, VMEM],
        out_specs=VMEM,
        compiler_params=near,
        name="pool",
    )(window_map, pool_segments, keys_p, values_p)
    other = lax.ppermute(pooled, "zh", SWAP)
    piece = lax.dynamic_index_in_dim(spread, owner_x, 0, keepdims=False)
    piece = piece.reshape(n_head, 2 * part, half)
    piece = jnp.broadcast_to(piece[None], (n_zh, n_head, 2 * part, half))
    piece, pooled, other = tie((piece, pooled, other))

    turned = lax.all_to_all(
        piece.reshape(n_zh * n_head, 2 * part, half), ("zh", "head"), 0, 0, tiled=True
    )
    pooled = jnp.concatenate([pooled, other], axis=0)
    other = lax.ppermute(pooled, "x", [(i, i ^ 1) for i in range(n_x)])
    pooled = jnp.concatenate([pooled, other], axis=0)
    turned = turned.reshape(n_zh, n_head * 2 * part, half)
    block = lax.dynamic_index_in_dim(turned, owner_z, 0, keepdims=False)
    block = jnp.broadcast_to(block[None], (n_x, n_head * 2 * part, half))
    other = lax.ppermute(pooled, "x", [(i, i ^ 2) for i in range(n_x)])

    block, queries_w = tie((block, queries))

    own = lax.all_to_all(block, "x", 0, 0, tiled=True).reshape(-1, 2, part, half)
    pooled = jnp.concatenate([pooled, other], axis=0)
    other = lax.ppermute(pooled, "c", SWAP)
    acc_w, stat_w = pl.pallas_call(
        window_kernel,
        out_shape=state,
        in_specs=[VMEM] * 3,
        out_specs=(VMEM, VMEM),
        compiler_params=near,
        cost_estimate=pl.CostEstimate(
            flops=4 * rows * rows * width,
            bytes_accessed=10 * rows * width,
            transcendentals=rows * rows * heads,
        ),
        name="window",
    )(queries_w, keys, values)
    acc, stat = pl.pallas_call(
        pooled_kernel,
        out_shape=state,
        in_specs=[SMEM, SMEM] + [VMEM] * 5,
        out_specs=(VMEM, VMEM),
        compiler_params=near,
        cost_estimate=pl.CostEstimate(
            flops=8 * rows * pooled.shape[0] * width,
            bytes_accessed=12 * rows * width,
            transcendentals=2 * rows * pooled.shape[0] * heads,
        ),
        name="pooled",
    )(window_map, slopes, queries, pooled, other, acc_w, stat_w)
    own, stat = tie((own, stat))

    got = lax.ppermute(own, "c", SWAP)
    out = pl.pallas_call(
        own_kernel,
        out_shape=jax.ShapeDtypeStruct((rows, half), jnp.bfloat16),
        in_specs=[SMEM] + [VMEM] * 4,
        out_specs=VMEM,
        compiler_params=near,
        cost_estimate=pl.CostEstimate(
            flops=2 * rows * rows * width,
            bytes_accessed=5 * rows * width,
            transcendentals=rows * rows * heads // 2,
        ),
        name="own",
    )(side, queries, own, acc, stat)
    return pl.pallas_call(
        got_kernel,
        out_shape=jax.ShapeDtypeStruct((rows, width), jnp.bfloat16),
        in_specs=[SMEM] + [VMEM] * 5,
        out_specs=ANY,
        scratch_shapes=[
            pltpu.VMEM((rows, half), jnp.bfloat16),
            pltpu.SemaphoreType.DMA((half // HD + 1,)),
        ],
        compiler_params=near,
        name="got",
    )(side, queries, got, acc, stat, out)


def solution(mesh):
    shape = mesh.shape
    ctx = shape["ctx"]
    fine = Mesh(
        mesh.devices.reshape(shape["dp"], 2, ctx // 4, 2, shape["head"]),
        ("dp", "zh", "x", "c", "head"),
    )
    token = ("dp", "zh", "x", "c")
    return jax.shard_map(
        on_device,
        mesh=fine,
        in_specs=(
            P(token, "head"),
            P(token, "head"),
            P(token, "head"),
            P(token, None),
            P(token),
            P("dp"),
            P(token, "head", None),
            P(token, "head", None),
            P("head"),
        ),
        out_specs=P(token, "head"),
        check_vma=False,
    )
```

```python
import functools
import math

import jax
import jax.numpy as jnp
from jax import lax
from jax.experimental import pallas as pl
from jax.experimental.pallas import tpu as pltpu
from jax.sharding import Mesh, PartitionSpec as P

HD = 128
POOLS = 8
LOG2E = math.log2(math.e)
UNIT = LOG2E / math.sqrt(HD)
STRIP = 128
SWAP = [(0, 1), (1, 0)]


def dot_nt(a, b):
    return lax.dot_general(a, b, (((1,), (1,)), ((), ())), preferred_element_type=jnp.float32)


def dot_nn(a, b):
    return jnp.dot(a, b, preferred_element_type=jnp.float32)


def pool_kernel(tag_ref, seg_ref, key_ref, value_ref, out_ref):
    seg = seg_ref[...]
    member = seg == lax.broadcasted_iota(jnp.int32, (POOLS, seg.shape[1]), 0)
    count = jnp.sum(member.astype(jnp.float32), axis=1, keepdims=True)
    member = member.astype(jnp.float32).astype(jnp.bfloat16)
    width = key_ref.shape[1]
    out_ref[:, :width] = (dot_nn(member, key_ref[...]) / count).astype(jnp.bfloat16)
    out_ref[:, width : 2 * width] = (dot_nn(member, value_ref[...]) / count).astype(jnp.bfloat16)
    tag = jnp.full((POOLS, HD), tag_ref[0], jnp.int32)
    out_ref[:, 2 * width :] = tag.astype(jnp.float32).astype(jnp.bfloat16)


def soft(scores):
    top = jnp.max(scores, axis=0, keepdims=True)
    exp_terms = jnp.exp2(scores - top)
    return top, jnp.sum(exp_terms, axis=0, keepdims=True), exp_terms.astype(jnp.bfloat16)


def window_kernel(q_ref, k_ref, v_ref, acc_ref, stat_ref):
    for head in range(q_ref.shape[1] // HD):
        cols = pl.ds(head * HD, HD)
        values = v_ref[:, cols].T
        for start in range(0, q_ref.shape[0], STRIP):
            rows = pl.ds(start, STRIP)
            top, total, weights = soft(dot_nt(k_ref[:, cols], q_ref[rows, cols]) * UNIT)
            acc_ref[cols, rows] = dot_nn(values, weights)
            stat_ref[2 * head : 2 * head + 1, rows] = top
            stat_ref[2 * head + 1 : 2 * head + 2, rows] = total


def pooled_kernel(
    tag_ref, slope_ref, q_ref, pa_ref, pb_ref, acc_ref, stat_ref, acc_out_ref, stat_out_ref
):
    count, width = q_ref.shape

    def both(first):
        cols = pl.ds(first, HD)
        return jnp.concatenate([pa_ref[:, cols], pb_ref[:, cols]], axis=0)

    tags = both(2 * width).astype(jnp.float32)
    dist = jnp.abs(tags - tag_ref[0].astype(jnp.float32)) * LOG2E
    dist = jnp.concatenate([dist] * (count // HD), axis=1)
    for head in range(width // HD):
        cols = pl.ds(head * HD, HD)
        scores = dot_nt(both(head * HD), q_ref[:, cols]) * UNIT - dist * slope_ref[head]
        top, total, weights = soft(scores)
        num = dot_nn(both(width + head * HD).T, weights)
        top_n = stat_ref[2 * head : 2 * head + 1, :]
        total_n = stat_ref[2 * head + 1 : 2 * head + 2, :]
        ceiling = jnp.maximum(top_n, top)
        share_n, share = jnp.exp2(top_n - ceiling), jnp.exp2(top - ceiling)
        acc_out_ref[cols, :] = share_n * acc_ref[cols, :] + share * num
        stat_out_ref[2 * head : 2 * head + 1, :] = ceiling
        stat_out_ref[2 * head + 1 : 2 * head + 2, :] = share_n * total_n + share * total


def split_kernel(side_ref, k_ref, v_ref, out_ref):
    groups, half = out_ref.shape[1], out_ref.shape[4]

    def move(side):
        for kind, src in enumerate((k_ref, v_ref)):
            for group in range(groups):
                out_ref[:, group, kind] = src[:, :, pl.ds((2 * group + side) * half, half)]

    for side in range(2):
        pl.when(side_ref[0] == side)(functools.partial(move, side))


def give_kernel(side_ref, k_ref, v_ref, out_ref, buf, in_sems, out_sems):
    groups, half = out_ref.shape[1], out_ref.shape[4]

    def move(side):
        pairs = [
            (
                pltpu.make_async_copy(
                    src.at[:, :, pl.ds((2 * group + side) * half, half)],
                    buf.at[:, group, kind],
                    in_sems.at[kind, group],
                ),
                pltpu.make_async_copy(
                    buf.at[:, group, kind], out_ref.at[:, group, kind], out_sems.at[kind, group]
                ),
            )
            for kind, src in enumerate((k_ref, v_ref))
            for group in range(groups)
        ]
        for fetch, _ in pairs:
            fetch.start()
        for fetch, store in pairs:
            fetch.wait()
            store.start()
        for _, store in pairs:
            store.wait()

    for side in range(2):
        pl.when(side_ref[0] == side)(functools.partial(move, side))


def ref_heads(q_ref, kv_ref, acc_ref, stat_ref, side, write):
    count = kv_ref.shape[3] // HD
    for local in range(count):
        head = side * count + local
        cols, lanes = pl.ds(head * HD, HD), pl.ds(local * HD, HD)
        keys = kv_ref[:, 0, :, lanes].reshape(-1, HD)
        values = kv_ref[:, 1, :, lanes].reshape(-1, HD).T
        for start in range(0, q_ref.shape[0], STRIP):
            rows = pl.ds(start, STRIP)
            top, total, weights = soft(dot_nt(keys, q_ref[rows, cols]) * UNIT)
            num = dot_nn(values, weights)
            top_n = stat_ref[2 * head : 2 * head + 1, rows]
            total_n = stat_ref[2 * head + 1 : 2 * head + 2, rows]
            ceiling = jnp.maximum(top_n, top)
            share_n, share = jnp.exp2(top_n - ceiling), jnp.exp2(top - ceiling)
            scale = 1.0 / (share_n * total_n + share * total)
            merged = (share_n * scale) * acc_ref[cols, rows] + (share * scale) * num
            write(rows, cols, lanes, merged.astype(jnp.bfloat16).T)


def own_kernel(core_ref, q_ref, kv_ref, acc_ref, stat_ref, part_ref):
    def write(rows, cols, lanes, block):
        part_ref[rows, lanes] = block

    for side in range(2):
        pl.when(core_ref[0] == side)(
            functools.partial(ref_heads, q_ref, kv_ref, acc_ref, stat_ref, side, write)
        )


def got_kernel(core_ref, q_ref, kv_ref, acc_ref, stat_ref, part_ref, out_ref, buf, sems):
    half = part_ref.shape[1]

    def finish(side):
        done = [
            pltpu.make_async_copy(
                part_ref, out_ref.at[:, pl.ds(side * half, half)], sems.at[half // HD]
            )
        ]
        done[0].start()

        def write(rows, cols, lanes, block):
            buf[rows, lanes] = block
            if rows.start + rows.size == buf.shape[0]:
                copy = pltpu.make_async_copy(
                    buf.at[:, lanes], out_ref.at[:, cols], sems.at[lanes.start // HD]
                )
                copy.start()
                done.append(copy)

        ref_heads(q_ref, kv_ref, acc_ref, stat_ref, 1 - side, write)
        for copy in done:
            copy.wait()

    for side in range(2):
        pl.when(core_ref[0] == side)(functools.partial(finish, side))


SMEM = pl.BlockSpec(memory_space=pltpu.SMEM)
VMEM = pl.BlockSpec(memory_space=pltpu.VMEM)
ANY = pl.BlockSpec(memory_space=pl.ANY)
GRANT = 63600 * 1024


def on_device(
    queries, keys, values, pool_segments, window_map, ref_owner, ref_keys, ref_values, slopes
):
    rows, width = queries.shape
    heads = width // HD
    n_zh, n_x, n_head = lax.axis_size("zh"), lax.axis_size("x"), lax.axis_size("head")
    ref_rows = ref_keys.shape[1]
    part = ref_rows // n_x
    core = lax.axis_index("c")
    owner = ref_owner[0]
    owner_c = owner % 2
    owner_x = (owner // 2) % n_x
    owner_z = owner // (2 * n_x)

    tie = lax.optimization_barrier
    near = pltpu.CompilerParams(vmem_limit_bytes=10 * 1024 * 1024)
    state = (
        jax.ShapeDtypeStruct((width, rows), jnp.float32),
        jax.ShapeDtypeStruct((16, rows), jnp.float32),
    )

    slot_k = ref_keys[0].reshape(n_x, part, -1)
    slot_v = ref_values[0].reshape(n_x, part, -1)
    half = width // 2
    side = core.astype(jnp.int32)[None]
    split = pl.pallas_call(
        split_kernel,
        out_shape=jax.ShapeDtypeStruct((n_x, n_head, 2, part, half), jnp.bfloat16),
        in_specs=[SMEM, VMEM, VMEM],
        out_specs=VMEM,
        compiler_params=near,
        name="split",
    )
    given = pl.pallas_call(
        give_kernel,
        out_shape=jax.ShapeDtypeStruct((n_x, n_head, 2, part, half), jnp.bfloat16),
        in_specs=[SMEM, ANY, ANY],
        out_specs=ANY,
        scratch_shapes=[
            pltpu.VMEM((n_x, n_head, 2, part, half), jnp.bfloat16),
            pltpu.SemaphoreType.DMA((2, n_head)),
            pltpu.SemaphoreType.DMA((2, n_head)),
        ],
        compiler_params=pltpu.CompilerParams(vmem_limit_bytes=GRANT),
        name="give",
    )(1 - side, slot_k, slot_v)
    got = lax.ppermute(given, "c", SWAP)
    given, slot_k, slot_v = tie((given, slot_k, slot_v))
    kept = tie(split(side, slot_k, slot_v))
    mine = jnp.where(owner_c == core, kept, got)
    mine, keys_p, values_p = tie((mine, keys, values))

    spread = lax.all_to_all(mine.reshape(n_x, -1, half), "x", 0, 0, tiled=True)
    pooled = pl.pallas_call(
        pool_kernel,
        out_shape=jax.ShapeDtypeStruct((POOLS, 2 * width + HD), jnp.bfloat16),
        in_specs=[SMEM, VMEM, VMEM, VMEM],
        out_specs=VMEM,
        compiler_params=near,
        name="pool",
    )(window_map, pool_segments, keys_p, values_p)
    other = lax.ppermute(pooled, "zh", SWAP)
    piece = lax.dynamic_index_in_dim(spread, owner_x, 0, keepdims=False)
    piece = piece.reshape(n_head, 2 * part, half)
    piece = jnp.broadcast_to(piece[None], (n_zh, n_head, 2 * part, half))
    piece, pooled, other = tie((piece, pooled, other))

    turned = lax.all_to_all(
        piece.reshape(n_zh * n_head, 2 * part, half), ("zh", "head"), 0, 0, tiled=True
    )
    pooled = jnp.concatenate([pooled, other], axis=0)
    other = lax.ppermute(pooled, "x", [(i, i ^ 2) for i in range(n_x)])
    pooled = jnp.concatenate([pooled, other], axis=0)
    turned = turned.reshape(n_zh, n_head * 2 * part, half)
    block = lax.dynamic_index_in_dim(turned, owner_z, 0, keepdims=False)
    block = jnp.broadcast_to(block[None], (n_x, n_head * 2 * part, half))
    other = lax.ppermute(pooled, "x", [(i, i ^ 1) for i in range(n_x)])

    block, queries_w = tie((block, queries))

    own = lax.all_to_all(block, "x", 0, 0, tiled=True).reshape(-1, 2, part, half)
    pooled = jnp.concatenate([pooled, other], axis=0)
    other = lax.ppermute(pooled, "c", SWAP)
    acc_w, stat_w = pl.pallas_call(
        window_kernel,
        out_shape=state,
        in_specs=[VMEM] * 3,
        out_specs=(VMEM, VMEM),
        compiler_params=near,
        cost_estimate=pl.CostEstimate(
            flops=4 * rows * rows * width,
            bytes_accessed=10 * rows * width,
            transcendentals=rows * rows * heads,
        ),
        name="window",
    )(queries_w, keys, values)
    acc, stat = pl.pallas_call(
        pooled_kernel,
        out_shape=state,
        in_specs=[SMEM, SMEM] + [VMEM] * 5,
        out_specs=(VMEM, VMEM),
        compiler_params=near,
        cost_estimate=pl.CostEstimate(
            flops=8 * rows * pooled.shape[0] * width,
            bytes_accessed=12 * rows * width,
            transcendentals=2 * rows * pooled.shape[0] * heads,
        ),
        name="pooled",
    )(window_map, slopes, queries, pooled, other, acc_w, stat_w)
    own, stat = tie((own, stat))

    got = lax.ppermute(own, "c", SWAP)
    out = pl.pallas_call(
        own_kernel,
        out_shape=jax.ShapeDtypeStruct((rows, half), jnp.bfloat16),
        in_specs=[SMEM] + [VMEM] * 4,
        out_specs=VMEM,
        compiler_params=near,
        cost_estimate=pl.CostEstimate(
            flops=2 * rows * rows * width,
            bytes_accessed=5 * rows * width,
            transcendentals=rows * rows * heads // 2,
        ),
        name="own",
    )(side, queries, own, acc, stat)
    return pl.pallas_call(
        got_kernel,
        out_shape=jax.ShapeDtypeStruct((rows, width), jnp.bfloat16),
        in_specs=[SMEM] + [VMEM] * 5,
        out_specs=ANY,
        scratch_shapes=[
            pltpu.VMEM((rows, half), jnp.bfloat16),
            pltpu.SemaphoreType.DMA((half // HD + 1,)),
        ],
        compiler_params=near,
        name="got",
    )(side, queries, got, acc, stat, out)


def solution(mesh):
    shape = mesh.shape
    ctx = shape["ctx"]
    fine = Mesh(
        mesh.devices.reshape(shape["dp"], 2, ctx // 4, 2, shape["head"]),
        ("dp", "zh", "x", "c", "head"),
    )
    token = ("dp", "zh", "x", "c")
    return jax.shard_map(
        on_device,
        mesh=fine,
        in_specs=(
            P(token, "head"),
            P(token, "head"),
            P(token, "head"),
            P(token, None),
            P(token),
            P("dp"),
            P(token, "head", None),
            P(token, "head", None),
            P("head"),
        ),
        out_specs=P(token, "head"),
        check_vma=False,
    )
```

```python
import functools
import math

import jax
import jax.numpy as jnp
from jax import lax
from jax.experimental import pallas as pl
from jax.experimental.pallas import tpu as pltpu
from jax.sharding import Mesh, PartitionSpec as P

HD = 128
POOLS = 8
LOG2E = math.log2(math.e)
UNIT = LOG2E / math.sqrt(HD)
STRIP = 128
SWAP = [(0, 1), (1, 0)]


def dot_nt(a, b):
    return lax.dot_general(a, b, (((1,), (1,)), ((), ())), preferred_element_type=jnp.float32)


def dot_nn(a, b):
    return jnp.dot(a, b, preferred_element_type=jnp.float32)


def pool_kernel(tag_ref, seg_ref, key_ref, value_ref, out_ref):
    seg = seg_ref[...]
    member = seg == lax.broadcasted_iota(jnp.int32, (POOLS, seg.shape[1]), 0)
    count = jnp.sum(member.astype(jnp.float32), axis=1, keepdims=True)
    member = member.astype(jnp.float32).astype(jnp.bfloat16)
    width = key_ref.shape[1]
    out_ref[:, :width] = (dot_nn(member, key_ref[...]) / count).astype(jnp.bfloat16)
    out_ref[:, width : 2 * width] = (dot_nn(member, value_ref[...]) / count).astype(jnp.bfloat16)
    tag = jnp.full((POOLS, HD), tag_ref[0], jnp.int32)
    out_ref[:, 2 * width :] = tag.astype(jnp.float32).astype(jnp.bfloat16)


def soft(scores):
    top = jnp.max(scores, axis=0, keepdims=True)
    exp_terms = jnp.exp2(scores - top)
    return top, jnp.sum(exp_terms, axis=0, keepdims=True), exp_terms.astype(jnp.bfloat16)


def window_kernel(q_ref, k_ref, v_ref, acc_ref, stat_ref):
    for head in range(q_ref.shape[1] // HD):
        cols = pl.ds(head * HD, HD)
        values = v_ref[:, cols].T
        for start in range(0, q_ref.shape[0], STRIP):
            rows = pl.ds(start, STRIP)
            top, total, weights = soft(dot_nt(k_ref[:, cols], q_ref[rows, cols]) * UNIT)
            acc_ref[cols, rows] = dot_nn(values, weights)
            stat_ref[2 * head : 2 * head + 1, rows] = top
            stat_ref[2 * head + 1 : 2 * head + 2, rows] = total


def pooled_kernel(
    tag_ref, slope_ref, q_ref, pa_ref, pb_ref, acc_ref, stat_ref, acc_out_ref, stat_out_ref
):
    count, width = q_ref.shape

    def both(first):
        cols = pl.ds(first, HD)
        return jnp.concatenate([pa_ref[:, cols], pb_ref[:, cols]], axis=0)

    tags = both(2 * width).astype(jnp.float32)
    dist = jnp.abs(tags - tag_ref[0].astype(jnp.float32)) * LOG2E
    dist = jnp.concatenate([dist] * (count // HD), axis=1)
    for head in range(width // HD):
        cols = pl.ds(head * HD, HD)
        scores = dot_nt(both(head * HD), q_ref[:, cols]) * UNIT - dist * slope_ref[head]
        top, total, weights = soft(scores)
        num = dot_nn(both(width + head * HD).T, weights)
        top_n = stat_ref[2 * head : 2 * head + 1, :]
        total_n = stat_ref[2 * head + 1 : 2 * head + 2, :]
        ceiling = jnp.maximum(top_n, top)
        share_n, share = jnp.exp2(top_n - ceiling), jnp.exp2(top - ceiling)
        acc_out_ref[cols, :] = share_n * acc_ref[cols, :] + share * num
        stat_out_ref[2 * head : 2 * head + 1, :] = ceiling
        stat_out_ref[2 * head + 1 : 2 * head + 2, :] = share_n * total_n + share * total


def split_kernel(side_ref, k_ref, v_ref, out_ref):
    groups, half = out_ref.shape[1], out_ref.shape[4]

    def move(side):
        for kind, src in enumerate((k_ref, v_ref)):
            for group in range(groups):
                out_ref[:, group, kind] = src[:, :, pl.ds((2 * group + side) * half, half)]

    for side in range(2):
        pl.when(side_ref[0] == side)(functools.partial(move, side))


def ref_heads(q_ref, kv_ref, acc_ref, stat_ref, side, write):
    count = kv_ref.shape[3] // HD
    for local in range(count):
        head = side * count + local
        cols, lanes = pl.ds(head * HD, HD), pl.ds(local * HD, HD)
        keys = kv_ref[:, 0, :, lanes].reshape(-1, HD)
        values = kv_ref[:, 1, :, lanes].reshape(-1, HD).T
        for start in range(0, q_ref.shape[0], STRIP):
            rows = pl.ds(start, STRIP)
            top, total, weights = soft(dot_nt(keys, q_ref[rows, cols]) * UNIT)
            num = dot_nn(values, weights)
            top_n = stat_ref[2 * head : 2 * head + 1, rows]
            total_n = stat_ref[2 * head + 1 : 2 * head + 2, rows]
            ceiling = jnp.maximum(top_n, top)
            share_n, share = jnp.exp2(top_n - ceiling), jnp.exp2(top - ceiling)
            scale = 1.0 / (share_n * total_n + share * total)
            merged = (share_n * scale) * acc_ref[cols, rows] + (share * scale) * num
            write(rows, cols, lanes, merged.astype(jnp.bfloat16).T)


def own_kernel(core_ref, q_ref, kv_ref, acc_ref, stat_ref, part_ref):
    def write(rows, cols, lanes, block):
        part_ref[rows, lanes] = block

    for side in range(2):
        pl.when(core_ref[0] == side)(
            functools.partial(ref_heads, q_ref, kv_ref, acc_ref, stat_ref, side, write)
        )


def got_kernel(core_ref, q_ref, kv_ref, acc_ref, stat_ref, part_ref, out_ref, buf, sems):
    half = part_ref.shape[1]

    def finish(side):
        done = [
            pltpu.make_async_copy(
                part_ref, out_ref.at[:, pl.ds(side * half, half)], sems.at[half // HD]
            )
        ]
        done[0].start()

        def write(rows, cols, lanes, block):
            buf[rows, lanes] = block
            if rows.start + rows.size == buf.shape[0]:
                copy = pltpu.make_async_copy(
                    buf.at[:, lanes], out_ref.at[:, cols], sems.at[lanes.start // HD]
                )
                copy.start()
                done.append(copy)

        ref_heads(q_ref, kv_ref, acc_ref, stat_ref, 1 - side, write)
        for copy in done:
            copy.wait()

    for side in range(2):
        pl.when(core_ref[0] == side)(functools.partial(finish, side))


SMEM = pl.BlockSpec(memory_space=pltpu.SMEM)
VMEM = pl.BlockSpec(memory_space=pltpu.VMEM)
ANY = pl.BlockSpec(memory_space=pl.ANY)


def on_device(
    queries, keys, values, pool_segments, window_map, ref_owner, ref_keys, ref_values, slopes
):
    rows, width = queries.shape
    heads = width // HD
    n_zh, n_x, n_head = lax.axis_size("zh"), lax.axis_size("x"), lax.axis_size("head")
    ref_rows = ref_keys.shape[1]
    part = ref_rows // n_x
    core = lax.axis_index("c")
    owner = ref_owner[0]
    owner_c = owner % 2
    owner_x = (owner // 2) % n_x
    owner_z = owner // (2 * n_x)

    tie = lax.optimization_barrier
    near = pltpu.CompilerParams(vmem_limit_bytes=10 * 1024 * 1024)
    state = (
        jax.ShapeDtypeStruct((width, rows), jnp.float32),
        jax.ShapeDtypeStruct((16, rows), jnp.float32),
    )

    slot_k = ref_keys[0].reshape(n_x, part, -1)
    slot_v = ref_values[0].reshape(n_x, part, -1)
    half = width // 2
    side = core.astype(jnp.int32)[None]
    split = pl.pallas_call(
        split_kernel,
        out_shape=jax.ShapeDtypeStruct((n_x, n_head, 2, part, half), jnp.bfloat16),
        in_specs=[SMEM, VMEM, VMEM],
        out_specs=VMEM,
        compiler_params=near,
        name="split",
    )
    given = split(1 - side, slot_k, slot_v)
    got = lax.ppermute(given, "c", SWAP)
    given, slot_k, slot_v = tie((given, slot_k, slot_v))
    kept = tie(split(side, slot_k, slot_v))
    mine = jnp.where(owner_c == core, kept, got)
    mine, keys_p, values_p = tie((mine, keys, values))

    spread = lax.all_to_all(mine.reshape(n_x, -1, half), "x", 0, 0, tiled=True)
    pooled = pl.pallas_call(
        pool_kernel,
        out_shape=jax.ShapeDtypeStruct((POOLS, 2 * width + HD), jnp.bfloat16),
        in_specs=[SMEM, VMEM, VMEM, VMEM],
        out_specs=VMEM,
        compiler_params=near,
        name="pool",
    )(window_map, pool_segments, keys_p, values_p)
    other = lax.ppermute(pooled, "zh", SWAP)
    piece = lax.dynamic_index_in_dim(spread, owner_x, 0, keepdims=False)
    piece = piece.reshape(n_head, 2 * part, half)
    piece = jnp.broadcast_to(piece[None], (n_zh, n_head, 2 * part, half))
    piece, pooled, other = tie((piece, pooled, other))

    turned = lax.all_to_all(
        piece.reshape(n_zh * n_head, 2 * part, half), ("zh", "head"), 0, 0, tiled=True
    )
    pooled = jnp.concatenate([pooled, other], axis=0)
    other = lax.ppermute(pooled, "x", [(i, i ^ 1) for i in range(n_x)])
    pooled = jnp.concatenate([pooled, other], axis=0)
    turned = turned.reshape(n_zh, n_head * 2 * part, half)
    block = lax.dynamic_index_in_dim(turned, owner_z, 0, keepdims=False)
    block = jnp.broadcast_to(block[None], (n_x, n_head * 2 * part, half))
    other = lax.ppermute(pooled, "x", [(i, i ^ 2) for i in range(n_x)])

    block, queries_w = tie((block, queries))

    own = lax.all_to_all(block, "x", 0, 0, tiled=True).reshape(-1, 2, part, half)
    pooled = jnp.concatenate([pooled, other], axis=0)
    other = lax.ppermute(pooled, "c", SWAP)
    acc_w, stat_w = pl.pallas_call(
        window_kernel,
        out_shape=state,
        in_specs=[VMEM] * 3,
        out_specs=(VMEM, VMEM),
        compiler_params=near,
        cost_estimate=pl.CostEstimate(
            flops=4 * rows * rows * width,
            bytes_accessed=10 * rows * width,
            transcendentals=rows * rows * heads,
        ),
        name="window",
    )(queries_w, keys, values)
    acc, stat = pl.pallas_call(
        pooled_kernel,
        out_shape=state,
        in_specs=[SMEM, SMEM] + [VMEM] * 5,
        out_specs=(VMEM, VMEM),
        compiler_params=near,
        cost_estimate=pl.CostEstimate(
            flops=8 * rows * pooled.shape[0] * width,
            bytes_accessed=12 * rows * width,
            transcendentals=2 * rows * pooled.shape[0] * heads,
        ),
        name="pooled",
    )(window_map, slopes, queries, pooled, other, acc_w, stat_w)
    own, stat = tie((own, stat))

    got = lax.ppermute(own, "c", SWAP)
    out = pl.pallas_call(
        own_kernel,
        out_shape=jax.ShapeDtypeStruct((rows, half), jnp.bfloat16),
        in_specs=[SMEM] + [VMEM] * 4,
        out_specs=VMEM,
        compiler_params=near,
        cost_estimate=pl.CostEstimate(
            flops=2 * rows * rows * width,
            bytes_accessed=5 * rows * width,
            transcendentals=rows * rows * heads // 2,
        ),
        name="own",
    )(side, queries, own, acc, stat)
    return pl.pallas_call(
        got_kernel,
        out_shape=jax.ShapeDtypeStruct((rows, width), jnp.bfloat16),
        in_specs=[SMEM] + [VMEM] * 5,
        out_specs=ANY,
        scratch_shapes=[
            pltpu.VMEM((rows, half), jnp.bfloat16),
            pltpu.SemaphoreType.DMA((half // HD + 1,)),
        ],
        compiler_params=near,
        name="got",
    )(side, queries, got, acc, stat, out)


def solution(mesh):
    shape = mesh.shape
    ctx = shape["ctx"]
    fine = Mesh(
        mesh.devices.reshape(shape["dp"], 2, ctx // 4, 2, shape["head"]),
        ("dp", "zh", "x", "c", "head"),
    )
    token = ("dp", "zh", "x", "c")
    return jax.shard_map(
        on_device,
        mesh=fine,
        in_specs=(
            P(token, "head"),
            P(token, "head"),
            P(token, "head"),
            P(token, None),
            P(token),
            P("dp"),
            P(token, "head", None),
            P(token, "head", None),
            P("head"),
        ),
        out_specs=P(token, "head"),
        check_vma=False,
    )
```
